128 devices in a mesh: row: 8 (over x_hi, z), col: 16 (over y, x_lo, core).
Axes of the slice: x: 4 (x_hi: 2, x_lo: 2; x = x_hi * 2 + x_lo), y: 4, z: 4, core: 2. Of those that a mesh axis runs over, the one named last changes fastest.
Arguments:
- a_blocks: float32 [2560, 64, 64], P(('row', 'col')), may hold values from -0.75 to 0.75
- a_rows: int32 [2560], P(('row', 'col')), may hold values from 0 to 15, as said below
- a_cols: int32 [2560], P(('row', 'col')), may hold values from 0 to 1023, as said below
- a_keep: int32 [2560], P(('row', 'col')), may hold values 0 or 1
- b_blocks: float32 [8192, 64, 64], P(('row', 'col')), may hold values from -0.75 to 0.75
- b_rows: int32 [8192], P(('row', 'col')), may hold values from 0 to 1023, as said below
- b_cols: int32 [8192], P(('row', 'col')), may hold values from 0 to 127, as said below
Outputs:
- c_panel: float32 [1024, 8192], P('row', 'col')
The draws below stay inside these ranges and needn't reach their ends.
Inputs may be any that keep to these rules, and one draw needn't show every extreme that they name: `a_rows`: the stored left blocks are laid out in 8 x 16 runs of 20, run d = r * 16 + c; run d holds blocks of block rows r * 2 to r * 2 + 1 only, no position twice. `a_cols`: run d = r * 16 + c of the left blocks has inner block indices c * 64 to c * 64 + 63 only. `b_rows`: the stored right blocks are laid out in runs of 64, run d = r * 16 + c; its first 32 blocks have inner block indices in group r (r * 64 to r * 64 + 63), the last 32 in group r + 8; no position twice. `b_cols`: run d = r * 16 + c of the right blocks has block columns c * 8 to c * 8 + 7 only.
All inputs are finite; a program needn't handle non-finite values. No bound on the sum of `a_keep` on one device may be relied on, other than what follows from the above.
Results may differ from the reference program's by a relative error of at most 0.0003.
Values sent between devices are 32-bit elements; how exact they have to be, the bound alone decides.
A program may use at most 192 MiB of HBM per device.

```python
import jax
import jax.numpy as jnp
from jax import lax

BS = 64
RW = 2
CW = 8
KG = 64
SA = 20
SB = 64
NRB = 16
NCB = 128
N_ROW = 8
N_COL = 16
DEVICES = 128


def left_positions(key):
    device_keys = jax.random.split(key, N_ROW * N_COL)
    return jax.vmap(lambda member: jax.random.permutation(member, RW * KG)[:SA])(device_keys).astype(jnp.int32)


def right_positions(key):
    key_right = jax.random.fold_in(key, 7)
    device_keys = jax.random.split(key_right, N_ROW * N_COL * 2)
    chosen = jax.vmap(lambda member: jax.random.permutation(member, KG * CW)[:SB // 2])(device_keys)
    return chosen.reshape(N_ROW * N_COL, 2, SB // 2).astype(jnp.int32)


def draw_a_rows(key, part):
    positions = left_positions(key)
    device_rows = (jnp.arange(N_ROW * N_COL, dtype=jnp.int32) // N_COL)[:, None]
    return (device_rows * RW + positions // KG).reshape(-1).astype(jnp.int32)


def draw_a_cols(key, part):
    positions = left_positions(key)
    device_cols = (jnp.arange(N_ROW * N_COL, dtype=jnp.int32) % N_COL)[:, None]
    return (device_cols * KG + positions % KG).reshape(-1).astype(jnp.int32)


def draw_b_rows(key, part):
    positions = right_positions(key)
    device_rows = (jnp.arange(N_ROW * N_COL, dtype=jnp.int32) // N_COL)[:, None, None]
    halves = jnp.arange(2, dtype=jnp.int32)[None, :, None]
    return ((halves * N_ROW + device_rows) * KG + positions // CW).reshape(-1).astype(jnp.int32)


def draw_b_cols(key, part):
    positions = right_positions(key)
    device_cols = (jnp.arange(N_ROW * N_COL, dtype=jnp.int32) % N_COL)[:, None, None]
    return (device_cols * CW + positions % CW).reshape(-1).astype(jnp.int32)


def set_ends(array, key, low, high):
    spot = [jax.random.randint(jax.random.fold_in(key, axis), (), 0, length) for axis, length in enumerate(array.shape)]
    main_axis = array.shape.index(max(array.shape))
    beside = spot[:main_axis] + [(spot[main_axis] + 1) % array.shape[main_axis]] + spot[main_axis + 1:]
    return array.at[tuple(spot)].set(low).at[tuple(beside)].set(high)


def steps_of(key, shape, cuts, smallest, top_value):
    loudness = 1.0
    for axis_at, parts in cuts:
        draws = jax.random.uniform(jax.random.fold_in(jax.random.fold_in(key, 6), axis_at), (parts,), jnp.float32, smallest / len(cuts), top_value / len(cuts))
        loudness = loudness * jnp.repeat(jnp.exp(draws), shape[axis_at] // parts).reshape((-1,) + (1,) * (len(shape) - 1 - axis_at))
    return loudness


def bell_draw(key, dims, width, reach, shards=(), held_as=jnp.bfloat16):
    result = width * jax.random.normal(key, dims, jnp.float32)
    if shards:
        result = result * steps_of(key, dims, shards, -0.22, 0.18)
    return jnp.clip(result, -reach, reach).astype(held_as)


def setup_inputs(seed: int = 0) -> dict:
    keys = jax.random.split(jax.random.key(seed), 8)
    return {
        "a_blocks": bell_draw(keys[0], (DEVICES * SA, BS, BS), 0.125, 0.75, ((0, 128),), jnp.float32),
        "a_rows": draw_a_rows(jax.random.fold_in(keys[7], 71), 0),
        "a_cols": draw_a_cols(jax.random.fold_in(keys[7], 71), 0),
        "a_keep": set_ends((jax.random.randint(keys[3], (DEVICES * SA,), 0, 8) < 7).astype(jnp.int32), jax.random.fold_in(keys[3], 1), 0, 1),
        "b_blocks": bell_draw(keys[4], (DEVICES * SB, BS, BS), 0.125, 0.75, ((0, 128),), jnp.float32),
        "b_rows": draw_b_rows(jax.random.fold_in(keys[7], 71), 0),
        "b_cols": draw_b_cols(jax.random.fold_in(keys[7], 71), 0),
    }


def reference(a_blocks, a_rows, a_cols, a_keep, b_blocks, b_rows, b_cols):
    half_slots = SB // 2
    kept = a_blocks * a_keep.astype(a_blocks.dtype)[:, None, None]
    left_grouped = kept.reshape(N_ROW, N_COL, SA, BS, BS).transpose(1, 0, 2, 3, 4).reshape(N_COL, N_ROW * SA, BS, BS)
    left_rows = a_rows.reshape(N_ROW, N_COL, SA).transpose(1, 0, 2).reshape(N_COL, N_ROW * SA)
    left_cols = a_cols.reshape(N_ROW, N_COL, SA).transpose(1, 0, 2).reshape(N_COL, N_ROW * SA)
    right_grouped = b_blocks.reshape(N_ROW, N_COL, 2, half_slots, BS, BS).transpose(2, 0, 1, 3, 4, 5).reshape(N_COL, N_COL * half_slots, BS, BS)
    right_rows = b_rows.reshape(N_ROW, N_COL, 2, half_slots).transpose(2, 0, 1, 3).reshape(N_COL, N_COL * half_slots)
    right_cols = b_cols.reshape(N_ROW, N_COL, 2, half_slots).transpose(2, 0, 1, 3).reshape(N_COL, N_COL * half_slots)
    slot_total = N_ROW * SA
    group_size = 32 if slot_total % 32 == 0 else slot_total

    def one_group(accum_c, members):
        k_group, left_blk, left_row, left_col, right_blk, right_row, right_col = members
        k_first = k_group * KG
        dense_b = jnp.zeros((KG, BS, NCB, BS), right_blk.dtype)
        dense_b = dense_b.at[right_row - k_first, :, right_col, :].add(right_blk)
        dense_b = dense_b.reshape(KG, BS, NCB * BS)
        row_ids = jnp.arange(NRB, dtype=jnp.int32)

        def absorb(partial_value, pieces):
            blk, krow, brow = pieces
            stripes = jnp.take(dense_b, krow - k_first, axis=0)
            products = jnp.einsum("gxy,gyz->gxz", blk, stripes, precision=lax.Precision.HIGHEST)
            onehot = (brow[None, :] == row_ids[:, None]).astype(blk.dtype)
            return partial_value + jnp.einsum("rg,gxz->rxz", onehot, products, precision=lax.Precision.HIGHEST), None

        stacked = (left_blk.reshape(-1, group_size, BS, BS), left_col.reshape(-1, group_size), left_row.reshape(-1, group_size))
        accum_c, _ = lax.scan(absorb, accum_c, stacked)
        return accum_c, None

    start_c = jnp.zeros((NRB, BS, NCB * BS), a_blocks.dtype)
    groups = jnp.arange(N_COL, dtype=jnp.int32)
    accum_c, _ = lax.scan(one_group, start_c, (groups, left_grouped, left_rows, left_cols, right_grouped, right_rows, right_cols))
    return accum_c.reshape(NRB * BS, NCB * BS)
```

```python
import functools

import jax
import jax.numpy as jnp
from jax import lax
from jax.experimental import pallas as pl
from jax.experimental.pallas import tpu as pltpu
from jax.sharding import PartitionSpec as P

MESH = pl.DeviceIdType.MESH
BS = 64
KG = 64
RW = 2
CW = 8
SA = 20
SB = 64
PAIRS = SA // 2
ROWS = PAIRS * BS
PIECE = ROWS // 16
SEG = 2 * PIECE
PLANE = ROWS // 2
CHUNKS = 8
F32 = jnp.float32
BF16 = jnp.bfloat16


def split(value):
    high = value.astype(BF16)
    low = (value - high.astype(F32)).astype(BF16)
    return high, low


def kernel(
    a_rows, a_cols, a_keep, b_rows, b_cols, a_hbm, b_hbm, out,
    a_raw, packed, a_all, b_raw, left_hi, left_lo, right_hi, right_lo, dense_hi, dense_lo,
    meta_out, meta_in, meta_rows, meta_s, table_v, table_s,
    c_part, c_z, c_x_out, c_x_in,
    load_sem, smem_sem, scat_send, scat_recv, meta_send, meta_recv,
    x_send, x_recv, y_send, y_recv, f_send, f_recv, core_send, core_recv,
    z_send, z_recv, h_send, h_recv,
):
    r = lax.axis_index("row")
    c = lax.axis_index("col")
    x_hi, z = r // 4, r % 4
    y, x_lo, core = c // 4, (c // 2) % 2, c % 2
    kappa, half = c % 8, c // 8
    local_target = kappa == r
    sibling = (r, y * 4 + x_lo * 2 + (1 - core))
    x_near = (r, y * 4 + (1 - x_lo) * 2 + core)
    y_up = (r, ((y + 1) % 4) * 4 + x_lo * 2 + core)
    y_down = (r, ((y + 3) % 4) * 4 + x_lo * 2 + core)
    x_far = ((1 - x_hi) * 4 + z, c)
    z_peer = [(x_hi * 4 + (z + d) % 4, c) for d in range(4)]

    load_b = pltpu.make_async_copy(b_hbm, b_raw, load_sem.at[1])
    load_a = pltpu.make_async_copy(a_hbm, a_raw, load_sem.at[0])
    load_a.start()
    load_b.start()

    barrier = pltpu.get_barrier_semaphore()
    for peer in (sibling, x_near, y_up, y_down, x_far, z_peer[1], z_peer[2], z_peer[3]):
        pl.semaphore_signal(barrier, inc=1, device_id=peer, device_id_type=MESH)

    def greet(i, carry):
        source = (i // 2, r + 8 * (i % 2))

        @pl.when(jnp.logical_or(source[0] != r, source[1] != c))
        def _():
            pl.semaphore_signal(barrier, inc=1, device_id=source, device_id_type=MESH)

        return carry

    lax.fori_loop(0, 16, greet, 0)

    lane = lax.broadcasted_iota(jnp.int32, (8, 128), 1)
    sub = lax.broadcasted_iota(jnp.int32, (8, 128), 0)
    meta = jnp.zeros((8, 128), jnp.int32)
    for a in range(SA):
        keep = a_keep[a]
        low_row = lax.rem(a_rows[a], RW)
        meta = jnp.where(lane == a, lax.rem(a_cols[a], KG) + half * KG, meta)
        meta = jnp.where(lane == 32 + a, keep * (1 - low_row), meta)
        meta = jnp.where(lane == 64 + a, keep * low_row, meta)
    meta_out[...] = meta

    load_a.wait()
    for p in range(PAIRS):
        packed[pl.ds(p * BS, BS), :] = jnp.concatenate([a_raw[2 * p], a_raw[2 * p + 1]], axis=1)

    @pl.when(local_target)
    def _():
        pl.semaphore_wait(barrier, 23)

    @pl.when(jnp.logical_not(local_target))
    def _():
        pl.semaphore_wait(barrier, 24)

    run = r * 2 + half

    def scatter(p, carry):
        target = (kappa, ((p // 2) % 4) * 4 + (p % 2) * 2 + p // 8)
        rows = pl.ds(pl.multiple_of(p * PIECE, 8), PIECE)
        here = jnp.logical_and(target[0] == r, target[1] == c)

        @pl.when(here)
        def _():
            pltpu.make_async_copy(packed.at[rows], a_all.at[run, rows], scat_recv.at[r]).start()
            pltpu.make_async_copy(meta_out, meta_in.at[run], meta_recv).start()

        @pl.when(jnp.logical_not(here))
        def _():
            pltpu.make_async_remote_copy(
                packed.at[rows], a_all.at[run, rows], scat_send, scat_recv.at[r],
                device_id=target, device_id_type=MESH,
            ).start()
            pltpu.make_async_remote_copy(
                meta_out, meta_in.at[run], meta_send, meta_recv,
                device_id=target, device_id_type=MESH,
            ).start()

        return carry

    lax.fori_loop(0, 16, scatter, 0)

    flat = sub * 128 + lane
    table = jnp.full((8, 128), SB, jnp.int32)
    for s in range(SB):
        inner = lax.rem(b_rows[s], KG) + (0 if s < SB // 2 else KG)
        place = inner * CW + lax.rem(b_cols[s], CW)
        table = jnp.where(flat == place, s, table)
    table_v[...] = table
    table_copy = pltpu.make_async_copy(table_v, table_s, smem_sem.at[0])
    table_copy.start()

    def chunk_of(t):
        return (x_hi + 1 - t // 4) % 2 * 4 + (z + t % 4 + 1) % 4

    own_rows = pl.ds(pl.multiple_of(core * PLANE + y * SEG + x_lo * PIECE, 8), PIECE)

    def seg_rows(where):
        return pl.ds(pl.multiple_of(core * PLANE + where * SEG, 8), SEG)

    def remote(src, dst, send, recv, peer):
        return pltpu.make_async_remote_copy(src, dst, send, recv, device_id=peer, device_id_type=MESH)

    def same(ref, send, recv, peer):
        return remote(ref, ref, send, recv, peer)

    def stage_x(t, carry):
        ch = chunk_of(t)
        mine = a_all.at[pl.ds(2 * ch, 2), own_rows]
        same(mine, x_send, scat_recv.at[ch], x_near).wait_recv()
        same(mine, x_send, x_recv.at[t], x_near).start()
        return carry

    def stage_y(t):
        ch = chunk_of(t)
        mine = a_all.at[pl.ds(2 * ch, 2), own_rows]
        same(mine, x_send, x_recv.at[t], x_near).wait_recv()
        seg = a_all.at[pl.ds(2 * ch, 2), seg_rows(y)]
        same(seg, y_send.at[0], y_recv.at[0, t], y_up).start()
        same(seg, y_send.at[1], y_recv.at[1, t], y_down).start()

    def stage_f(t):
        ch = chunk_of(t)
        below = a_all.at[pl.ds(2 * ch, 2), seg_rows((y + 3) % 4)]
        same(below, y_send.at[0], y_recv.at[0, t], y_up).wait_recv()
        half_below = a_all.at[2 * ch, seg_rows((y + 3) % 4)]
        same(half_below, f_send.at[0], f_recv.at[0, t], y_up).start()
        above = a_all.at[pl.ds(2 * ch, 2), seg_rows((y + 1) % 4)]
        same(above, y_send.at[1], y_recv.at[1, t], y_down).wait_recv()
        half_above = a_all.at[2 * ch + 1, seg_rows((y + 1) % 4)]
        same(half_above, f_send.at[1], f_recv.at[1, t], y_down).start()

    plane_rows = pl.ds(pl.multiple_of(core * PLANE, 8), PLANE)
    far_rows = seg_rows((y + 2) % 4)

    def stage_core(t):
        ch = chunk_of(t)
        same(a_all.at[2 * ch, far_rows], f_send.at[0], f_recv.at[0, t], y_up).wait_recv()
        same(a_all.at[2 * ch + 1, far_rows], f_send.at[1], f_recv.at[1, t], y_down).wait_recv()
        same(a_all.at[pl.ds(2 * ch, 2), plane_rows], core_send, core_recv.at[t], sibling).start()

    pair_lane = lax.broadcasted_iota(jnp.int32, (1, 128), 1) < BS

    def pair_mask(run_at, base, p):
        first = meta_s[run_at, base + 2 * p].astype(F32)
        second = meta_s[run_at, base + 2 * p + 1].astype(F32)
        return jnp.where(pair_lane, first, second)

    def stage_product(t):
        ch = chunk_of(t)
        same(a_all.at[pl.ds(2 * ch, 2), plane_rows], core_send, core_recv.at[t], sibling).wait_recv()
        total = jnp.zeros((RW * BS, CW * BS), F32)
        for h in range(2):
            at = 2 * ch + h
            for g in range(PAIRS // 2):
                block = jnp.concatenate(
                    [a_all[at, pl.ds((2 * g + i) * BS, BS), :] for i in range(2)], axis=1
                )
                high, low = split(block)
                masks = [
                    jnp.concatenate([pair_mask(at, base, 2 * g + i) for i in range(2)], axis=1).astype(BF16)
                    for base in (32, 64)
                ]
                left_high = jnp.concatenate([high * m for m in masks], axis=0)
                left_low = jnp.concatenate([low * m for m in masks], axis=0)
                inner = [meta_s[at, 4 * g + i] for i in range(4)]
                right_high = jnp.concatenate([dense_hi[k] for k in inner], axis=0)
                right_low = jnp.concatenate([dense_lo[k] for k in inner], axis=0)
                total += jnp.dot(left_high, right_high, preferred_element_type=F32)
                total += jnp.dot(left_low, right_high, preferred_element_type=F32)
                total += jnp.dot(left_high, right_low, preferred_element_type=F32)
        c_part[t] = total
        d = (t + 1) % 4

        @pl.when(d != 0)
        def _():
            remote(
                c_part.at[t], c_z.at[t], z_send.at[t], z_recv.at[t], (x_hi * 4 + (z + d) % 4, c)
            ).start()

    def build(k, carry):
        for j in range(CW // 2):
            first = table_s[k // 16, (k % 16) * CW + 2 * j]
            second = table_s[k // 16, (k % 16) * CW + 2 * j + 1]
            dense_hi[k, :, pl.ds(j * 128, 128)] = left_hi[first] + right_hi[second]
            dense_lo[k, :, pl.ds(j * 128, 128)] = left_lo[first] + right_lo[second]
        return carry

    load_b.wait()
    blank = jnp.zeros((BS, BS), F32)

    def widen(s, carry):
        value = b_raw[s]
        left_hi[s], left_lo[s] = split(jnp.concatenate([value, blank], axis=1))
        right_hi[s], right_lo[s] = split(jnp.concatenate([blank, value], axis=1))
        return carry

    lax.fori_loop(0, SB, widen, 0)
    for ref in (left_hi, left_lo, right_hi, right_lo):
        ref[SB] = jnp.zeros((BS, 2 * BS), BF16)

    lax.fori_loop(0, CHUNKS, stage_x, 0)
    table_copy.wait()
    stage_y(0)
    stage_y(1)
    lax.fori_loop(0, KG, build, 0)
    stage_f(0)
    lax.fori_loop(KG, 2 * KG, build, 0)

    pltpu.make_async_copy(meta_in, meta_in, meta_recv).wait()
    for i in range(16):
        meta_rows[pl.ds(i, 1), :] = meta_in[i, pl.ds(0, 1), :]
    meta_copy = pltpu.make_async_copy(meta_rows, meta_s, smem_sem.at[1])
    meta_copy.start()
    meta_copy.wait()

    def step(t, carry):
        @pl.when(t < CHUNKS - 2)
        def _():
            stage_y(t + 2)

        @pl.when(t < CHUNKS - 1)
        def _():
            stage_f(t + 1)

        @pl.when(t < CHUNKS)
        def _():
            stage_core(t)

        @pl.when(t > 0)
        def _():
            stage_product(t - 1)

        @pl.when(t == 6)
        def _():
            for i in range(3):
                remote(c_part.at[i], c_z.at[i], z_send.at[i], z_recv.at[i], x_far).wait_recv()
            c_x_out[...] = (c_part[3] + c_z[0]) + (c_z[1] + c_z[2])
            remote(c_x_out, c_x_in, h_send, h_recv, x_far).start()

        return carry

    lax.fori_loop(0, CHUNKS + 1, step, 0)

    for i in range(4, 7):
        remote(c_part.at[i], c_z.at[i], z_send.at[i], z_recv.at[i], x_far).wait_recv()
    mine = (c_part[7] + c_z[4]) + (c_z[5] + c_z[6])
    remote(c_x_out, c_x_in, h_send, h_recv, x_far).wait_recv()
    out[...] = mine + c_x_in[...]

    def sent(ref, sem):
        remote(ref, ref, sem, h_recv, x_far).wait_send()

    @pl.when(local_target)
    def _():
        sent(packed.at[pl.ds(0, ROWS - PIECE)], scat_send)
        sent(meta_in.at[pl.ds(0, 15)], meta_send)

    @pl.when(jnp.logical_not(local_target))
    def _():
        sent(packed, scat_send)
        sent(meta_in, meta_send)

    sent(a_all.at[:, own_rows], x_send)
    for i in range(2):
        sent(a_all.at[:, seg_rows(y)], y_send.at[i])
        sent(a_all.at[pl.ds(0, CHUNKS), seg_rows(y)], f_send.at[i])
    sent(a_all.at[:, plane_rows], core_send)
    for i in (0, 1, 2, 4, 5, 6):
        sent(c_part.at[i], z_send.at[i])
    sent(c_x_out, h_send)


def on_device(a_blocks, a_rows, a_cols, a_keep, b_blocks, b_rows, b_cols):
    dma = pltpu.SemaphoreType.DMA
    return pl.pallas_call(
        kernel,
        out_shape=jax.ShapeDtypeStruct((RW * BS, CW * BS), F32),
        in_specs=[pl.BlockSpec(memory_space=pltpu.SMEM)] * 5 + [pl.BlockSpec(memory_space=pl.ANY)] * 2,
        out_specs=pl.BlockSpec(memory_space=pltpu.VMEM),
        scratch_shapes=[
            pltpu.VMEM((SA, BS, BS), F32),
            pltpu.VMEM((ROWS, 128), F32),
            pltpu.VMEM((16, ROWS, 128), F32),
            pltpu.VMEM((SB, BS, BS), F32),
            pltpu.VMEM((SB + 1, BS, 128), BF16),
            pltpu.VMEM((SB + 1, BS, 128), BF16),
            pltpu.VMEM((SB + 1, BS, 128), BF16),
            pltpu.VMEM((SB + 1, BS, 128), BF16),
            pltpu.VMEM((2 * KG, BS, CW * BS), BF16),
            pltpu.VMEM((2 * KG, BS, CW * BS), BF16),
            pltpu.VMEM((8, 128), jnp.int32),
            pltpu.VMEM((16, 8, 128), jnp.int32),
            pltpu.VMEM((16, 128), jnp.int32),
            pltpu.SMEM((16, 128), jnp.int32),
            pltpu.VMEM((8, 128), jnp.int32),
            pltpu.SMEM((8, 128), jnp.int32),
            pltpu.VMEM((CHUNKS, RW * BS, CW * BS), F32),
            pltpu.VMEM((CHUNKS, RW * BS, CW * BS), F32),
            pltpu.VMEM((RW * BS, CW * BS), F32),
            pltpu.VMEM((RW * BS, CW * BS), F32),
            dma((2,)), dma((2,)), dma, dma((CHUNKS,)), dma, dma,
            dma, dma((CHUNKS,)), dma((2,)), dma((2, CHUNKS)), dma((2,)), dma((2, CHUNKS)),
            dma, dma((CHUNKS,)),
            dma((CHUNKS,)), dma((CHUNKS,)), dma, dma,
        ],
        compiler_params=pltpu.CompilerParams(
            collective_id=0, has_side_effects=True, vmem_limit_bytes=56 * 1024 * 1024
        ),
        cost_estimate=pl.CostEstimate(flops=2 * 3 * 1024 * 2560 * 512, bytes_accessed=8 << 20, transcendentals=0),
    )(a_rows, a_cols, a_keep, b_rows, b_cols, a_blocks, b_blocks)


def solution(mesh):
    in_specs = (
        P(("row", "col"), None, None),
        P(("row", "col")),
        P(("row", "col")),
        P(("row", "col")),
        P(("row", "col"), None, None),
        P(("row", "col")),
        P(("row", "col")),
    )
    return jax.shard_map(
        on_device, mesh=mesh, in_specs=in_specs, out_specs=P("row", "col"), check_vma=False
    )
```

```python
import functools

import jax
import jax.numpy as jnp
from jax import lax
from jax.experimental import pallas as pl
from jax.experimental.pallas import tpu as pltpu
from jax.sharding import PartitionSpec as P

MESH = pl.DeviceIdType.MESH
BS = 64
KG = 64
RW = 2
CW = 8
SA = 20
SB = 64
PAIRS = SA // 2
ROWS = PAIRS * BS
PIECE = ROWS // 8
HALF = PIECE // 2
CHUNKS = 8
LATE = 3
EARLY = CHUNKS - LATE
UNROLL = 2
F32 = jnp.float32
BF16 = jnp.bfloat16


def split(value):
    high = value.astype(BF16)
    low = (value - high.astype(F32)).astype(BF16)
    return high, low


def kernel(
    a_rows, a_cols, a_keep, b_rows, b_cols, a_hbm, b_hbm, out,
    a_raw, packed, a_all, b_raw, twice_hi, twice_lo, dense_hi, dense_lo,
    meta_out, meta_in, meta_v, meta_s, table_v, table_s,
    c_part, z_half, z_full, c_x_out, c_x_in,
    load_sem, smem_sem, scat_send, scat_recv, meta_send, meta_recv, meta_swap_send, meta_swap_recv,
    x_send, x_recv, own_send, own_recv, near_send, near_recv, pass_send, pass_half_send, pass_recv,
    core_send, core_recv, zh_send, zh_recv, zf_send, zf_recv, h_send, h_recv,
):
    r = lax.axis_index("row")
    c = lax.axis_index("col")
    x_hi, z = r // 4, r % 4
    y, x_lo, core = c // 4, (c // 2) % 2, c % 2
    kappa, half = c % 8, c // 8
    local_target = jnp.logical_and(kappa == r, half == core)
    sibling = (r, y * 4 + x_lo * 2 + (1 - core))
    x_near = (r, y * 4 + (1 - x_lo) * 2 + core)
    y_way = [(r, ((y + 1) % 4) * 4 + x_lo * 2 + core), (r, ((y + 3) % 4) * 4 + x_lo * 2 + core)]
    z_way = [(x_hi * 4 + (z + 1) % 4, c), (x_hi * 4 + (z + 3) % 4, c)]
    x_far = ((1 - x_hi) * 4 + z, c)

    barrier = pltpu.get_barrier_semaphore()

    def greet(i, carry):
        @pl.when(jnp.logical_or(i != r, r + 8 * core != c))
        def _():
            pl.semaphore_signal(barrier, inc=1, device_id=(i, r + 8 * core), device_id_type=MESH)

        return carry

    lax.fori_loop(0, 8, greet, 0)
    for peer in (x_far, *z_way, *y_way, x_near, sibling):
        pl.semaphore_signal(barrier, inc=1, device_id=peer, device_id_type=MESH)

    load_a = pltpu.make_async_copy(a_hbm, a_raw, load_sem.at[0])
    load_b = pltpu.make_async_copy(b_hbm, b_raw, load_sem.at[1])
    load_a.start()
    load_b.start()

    lane = lax.broadcasted_iota(jnp.int32, (8, 128), 1)
    sub = lax.broadcasted_iota(jnp.int32, (8, 128), 0)
    meta = jnp.zeros((8, 128), jnp.int32)
    for a in range(SA):
        keep = a_keep[a]
        low_row = lax.rem(a_rows[a], RW)
        meta = jnp.where(lane == a, lax.rem(a_cols[a], KG) + half * KG, meta)
        meta = jnp.where(lane == 32 + a, keep * (1 - low_row), meta)
        meta = jnp.where(lane == 64 + a, keep * low_row, meta)
    meta_out[...] = meta

    load_a.wait()
    for p in range(PAIRS):
        packed[pl.ds(p * BS, BS), :] = jnp.concatenate([a_raw[2 * p], a_raw[2 * p + 1]], axis=1)

    @pl.when(local_target)
    def _():
        pl.semaphore_wait(barrier, 14)

    @pl.when(jnp.logical_not(local_target))
    def _():
        pl.semaphore_wait(barrier, 15)

    run = r * 2 + half

    def remote(src, dst, send, recv, peer):
        return pltpu.make_async_remote_copy(src, dst, send, recv, device_id=peer, device_id_type=MESH)

    def same(ref, send, recv, peer):
        return remote(ref, ref, send, recv, peer)

    def scatter(p, carry):
        target = (kappa, (p // 2) * 4 + (p % 2) * 2 + half)
        piece = packed.at[pl.ds(pl.multiple_of(p * PIECE, 16), PIECE)]
        place = a_all.at[run, p // 2, p % 2]
        here = jnp.logical_and(target[0] == r, target[1] == c)

        @pl.when(here)
        def _():
            pltpu.make_async_copy(piece, place, scat_recv.at[r]).start()
            pltpu.make_async_copy(meta_out, meta_in.at[r], meta_recv).start()

        @pl.when(jnp.logical_not(here))
        def _():
            remote(piece, place, scat_send, scat_recv.at[r], target).start()
            remote(meta_out, meta_in.at[r], meta_send, meta_recv, target).start()

        return carry

    lax.fori_loop(0, 8, scatter, 0)

    flat = sub * 128 + lane
    table = jnp.full((8, 128), SB, jnp.int32)
    for s in range(SB):
        inner = lax.rem(b_rows[s], KG) + (0 if s < SB // 2 else KG)
        place = inner * CW + lax.rem(b_cols[s], CW)
        table = jnp.where(flat == place, s, table)
    table_v[...] = table
    table_copy = pltpu.make_async_copy(table_v, table_s, smem_sem.at[0])
    table_copy.start()

    def chunk_of(t):
        turn = t % 4
        away = (2 + turn + (turn // 2) * (5 - 2 * turn)) % 4
        return (x_hi + 1 - t // 4) % 2 * 4 + (z + away) % 4

    def plane(t):
        return a_all.at[2 * chunk_of(t) + core]

    def crosses_late(t):
        return t >= EARLY

    def own(t):
        return plane(t).at[y, x_lo]

    def stage_own(t):
        piece = own(t)
        same(piece, own_send.at[0], scat_recv.at[chunk_of(t)], x_near).wait_recv()
        for way in range(2):
            same(piece, own_send.at[way], own_recv.at[way, t], y_way[way]).start()
        if not crosses_late(t):
            same(piece, x_send.at[0], x_recv.at[t], x_near).start()

    def stage_near(t):
        if t < EARLY:
            piece = plane(t).at[y, 1 - x_lo]
            same(piece, x_send.at[0], x_recv.at[t], x_near).wait_recv()
            for way in range(2):
                same(piece, near_send.at[way], near_recv.at[way, t], y_way[way]).start()

    def stage_pass(t):
        below = plane(t).at[(y + 3) % 4]
        above = plane(t).at[(y + 1) % 4]
        if crosses_late(t):
            for way, column in ((0, below), (1, above)):
                piece = column.at[x_lo]
                same(piece, own_send.at[way], own_recv.at[way, t], y_way[way]).wait_recv()
                part = piece.at[pl.ds(way * HALF, HALF)]
                same(part, pass_half_send.at[way], pass_recv.at[way, t], y_way[way]).start()
        else:
            same(below.at[x_lo], own_send.at[0], own_recv.at[0, t], y_way[0]).wait_recv()
            same(below.at[x_lo], pass_send.at[0], pass_recv.at[0, t], y_way[0]).start()
            same(above.at[1 - x_lo], near_send.at[1], near_recv.at[1, t], y_way[1]).wait_recv()
            same(above.at[1 - x_lo], pass_send.at[1], pass_recv.at[1, t], y_way[1]).start()

    def to_sibling(t):
        same(plane(t), core_send, core_recv.at[t], sibling).start()

    def stage_far(t):
        far = plane(t).at[(y + 2) % 4]
        if crosses_late(t):
            for way in range(2):
                part = far.at[x_lo, pl.ds(way * HALF, HALF)]
                same(part, pass_half_send.at[way], pass_recv.at[way, t], y_way[way]).wait_recv()
            same(plane(t).at[:, x_lo], x_send.at[1], x_recv.at[t], x_near).start()
        else:
            above = plane(t).at[(y + 1) % 4]
            below = plane(t).at[(y + 3) % 4]
            same(above.at[x_lo], own_send.at[1], own_recv.at[1, t], y_way[1]).wait_recv()
            same(below.at[1 - x_lo], near_send.at[0], near_recv.at[0, t], y_way[0]).wait_recv()
            same(far.at[x_lo], pass_send.at[0], pass_recv.at[0, t], y_way[0]).wait_recv()
            same(far.at[1 - x_lo], pass_send.at[1], pass_recv.at[1, t], y_way[1]).wait_recv()
            to_sibling(t)

    def stage_late(t):
        same(plane(t).at[:, 1 - x_lo], x_send.at[1], x_recv.at[t], x_near).wait_recv()
        to_sibling(t)

    pair_lane = lax.broadcasted_iota(jnp.int32, (1, 128), 1) < BS

    def pair_mask(h, ch, base, p):
        first = meta_s[h, ch, base + 2 * p].astype(F32)
        second = meta_s[h, ch, base + 2 * p + 1].astype(F32)
        return jnp.where(pair_lane, first, second)

    def pair_rows(at, p):
        parts, start, end = [], p * BS, (p + 1) * BS
        while start < end:
            piece, offset = divmod(start, PIECE)
            count = min(end - start, PIECE - offset)
            parts.append(a_all[at, piece // 2, piece % 2, pl.ds(offset, count), :])
            start += count
        return jnp.concatenate(parts, axis=0)

    def stage_product(t):
        ch = chunk_of(t)
        same(a_all.at[2 * ch + 1 - core], core_send, core_recv.at[t], sibling).wait_recv()
        total = jnp.zeros((RW * BS, CW * BS), F32)
        for h in range(2):
            for g in range(PAIRS // 2):
                block = jnp.concatenate([pair_rows(2 * ch + h, 2 * g + i) for i in range(2)], axis=1)
                high, low = split(block)
                masks = [
                    jnp.concatenate([pair_mask(h, ch, base, 2 * g + i) for i in range(2)], axis=1).astype(BF16)
                    for base in (32, 64)
                ]
                left_high = jnp.concatenate([high * m for m in masks], axis=0)
                left_low = jnp.concatenate([low * m for m in masks], axis=0)
                inner = [meta_s[h, ch, 4 * g + i] for i in range(4)]
                right_high = jnp.concatenate([dense_hi[k] for k in inner], axis=0)
                right_low = jnp.concatenate([dense_lo[k] for k in inner], axis=0)
                total += jnp.dot(left_high, right_high, preferred_element_type=F32)
                total += jnp.dot(left_low, right_high, preferred_element_type=F32)
                total += jnp.dot(left_high, right_low, preferred_element_type=F32)
        c_part[t] = total

    def part_rows(way):
        return pl.ds(way * BS, BS)

    def z_farthest(e, way):
        return remote(
            c_part.at[4 * e, part_rows(way)], z_half.at[e, way],
            zh_send.at[e, way], zh_recv.at[e, way], z_way[way],
        )

    def z_next(e, way):
        return remote(
            c_part.at[4 * e + 2 - way], z_full.at[e, way],
            zf_send.at[e, way], zf_recv.at[e, way], z_way[way],
        )

    def sum_along(t):
        e = t // 4

        @pl.when(t % 4 == 0)
        def _():
            for way in range(2):
                z_farthest(e, way).start()

        @pl.when(t % 4 == 2)
        def _():
            for way in (1, 0):
                z_farthest(e, way).wait_recv()
                c_part[4 * e + 2 - way, part_rows(way), :] += z_half[e, way]
                z_next(e, way).start()

        @pl.when(t == 5)
        def _():
            for way in range(2):
                z_next(0, way).wait_recv()
            c_x_out[...] = c_part[3] + z_full[0, 0] + z_full[0, 1]
            remote(c_x_out, c_x_in, h_send, h_recv, x_far).start()

    first_half = lax.broadcasted_iota(jnp.int32, (BS, 2 * BS), 1) < BS

    def build(step, carry):
        for u in range(UNROLL):
            k = step * UNROLL + u
            slots = [table_s[k // 16, (k % 16) * CW + j] for j in range(CW)]
            for dense, twice in ((dense_hi, twice_hi), (dense_lo, twice_lo)):
                tiles = [
                    jnp.where(first_half, twice[slots[j]], twice[slots[j + 1]]) for j in range(0, CW, 2)
                ]
                dense[k] = jnp.concatenate(tiles, axis=1)
        return carry

    def build_some(start, end):
        lax.fori_loop(start // UNROLL, end // UNROLL, build, 0)

    load_b.wait()

    def widen(step, carry):
        for u in range(4):
            s = step * 4 + u
            value = b_raw[s]
            twice_hi[s], twice_lo[s] = split(jnp.concatenate([value, value], axis=1))
        return carry

    lax.fori_loop(0, SB // 4, widen, 0)
    for ref in (twice_hi, twice_lo):
        ref[SB] = jnp.zeros((BS, 2 * BS), BF16)

    late = range(EARLY, CHUNKS)
    def meta_pass_on():
        pltpu.make_async_copy(meta_in, meta_in, meta_recv).wait()
        for i in range(8):
            meta_v[core, pl.ds(i, 1), :] = meta_in[i, pl.ds(0, 1), :]
        same(meta_v.at[core], meta_swap_send, meta_swap_recv, sibling).start()

    meta_copy = pltpu.make_async_copy(meta_v, meta_s, smem_sem.at[1])

    def meta_take():
        same(meta_v.at[1 - core], meta_swap_send, meta_swap_recv, sibling).wait_recv()
        meta_copy.start()

    table_copy.wait()
    build_some(0, 64)
    stage_own(7)
    stage_own(5)
    stage_own(6)
    stage_own(4)
    stage_own(3)
    stage_own(1)
    stage_own(2)
    stage_own(0)
    meta_pass_on()
    stage_near(0)
    stage_near(1)
    build_some(64, 80)
    stage_pass(5)
    stage_pass(6)
    stage_pass(7)
    stage_near(2)
    stage_pass(0)
    build_some(80, 96)
    stage_near(3)
    stage_pass(1)
    build_some(96, 112)
    stage_far(5)
    stage_far(6)
    stage_far(7)
    build_some(112, 128)
    meta_take()
    stage_far(0)
    meta_copy.wait()

    def step(i, carry):
        for t in range(CHUNKS):
            @pl.when(i == t)
            def _():
                if t + 4 < EARLY:
                    stage_near(t + 4)
                if t + 2 < EARLY:
                    stage_pass(t + 2)
                if t + 1 < EARLY:
                    stage_far(t + 1)
                if t + 1 in late:
                    stage_late(t + 1)

        stage_product(i)
        sum_along(i)
        return carry

    lax.fori_loop(0, CHUNKS, step, 0)

    for way in range(2):
        z_next(1, way).wait_recv()
    mine = c_part[7] + z_full[1, 0] + z_full[1, 1]
    remote(c_x_out, c_x_in, h_send, h_recv, x_far).wait_recv()
    out[...] = mine + c_x_in[...]

    def sent(ref, sem):
        remote(ref, ref, sem, h_recv, x_far).wait_send()

    def some(count):
        return a_all.at[pl.ds(0, count), 0, 0]

    @pl.when(local_target)
    def _():
        sent(some(7), scat_send)
        sent(meta_in.at[pl.ds(0, 7)], meta_send)

    @pl.when(jnp.logical_not(local_target))
    def _():
        sent(some(8), scat_send)
        sent(meta_in, meta_send)

    sent(meta_v.at[core], meta_swap_send)
    sent(some(CHUNKS - LATE), x_send.at[0])
    sent(a_all.at[pl.ds(0, LATE), :, 0], x_send.at[1])
    for way in range(2):
        sent(some(CHUNKS), own_send.at[way])
        sent(some(CHUNKS - LATE), near_send.at[way])
        sent(some(CHUNKS - LATE), pass_send.at[way])
        sent(a_all.at[pl.ds(0, LATE), 0, 0, pl.ds(0, HALF)], pass_half_send.at[way])
        for e in range(2):
            z_farthest(e, way).wait_send()
            z_next(e, way).wait_send()
    sent(a_all.at[pl.ds(0, CHUNKS)], core_send)
    sent(c_x_out, h_send)


def on_device(a_blocks, a_rows, a_cols, a_keep, b_blocks, b_rows, b_cols):
    dma = pltpu.SemaphoreType.DMA
    return pl.pallas_call(
        kernel,
        out_shape=jax.ShapeDtypeStruct((RW * BS, CW * BS), F32),
        in_specs=[pl.BlockSpec(memory_space=pltpu.SMEM)] * 5 + [pl.BlockSpec(memory_space=pl.ANY)] * 2,
        out_specs=pl.BlockSpec(memory_space=pltpu.VMEM),
        scratch_shapes=[
            pltpu.VMEM((SA, BS, BS), F32),
            pltpu.VMEM((ROWS, 128), F32),
            pltpu.VMEM((16, 4, 2, PIECE, 128), F32),
            pltpu.VMEM((SB, BS, BS), F32),
            pltpu.VMEM((SB + 1, BS, 128), BF16),
            pltpu.VMEM((SB + 1, BS, 128), BF16),
            pltpu.VMEM((2 * KG, BS, CW * BS), BF16),
            pltpu.VMEM((2 * KG, BS, CW * BS), BF16),
            pltpu.VMEM((8, 128), jnp.int32),
            pltpu.VMEM((8, 8, 128), jnp.int32),
            pltpu.VMEM((2, 8, 128), jnp.int32),
            pltpu.SMEM((2, 8, 128), jnp.int32),
            pltpu.VMEM((8, 128), jnp.int32),
            pltpu.SMEM((8, 128), jnp.int32),
            pltpu.VMEM((CHUNKS, RW * BS, CW * BS), F32),
            pltpu.VMEM((2, 2, BS, CW * BS), F32),
            pltpu.VMEM((2, 2, RW * BS, CW * BS), F32),
            pltpu.VMEM((RW * BS, CW * BS), F32),
            pltpu.VMEM((RW * BS, CW * BS), F32),
            dma((2,)), dma((2,)), dma, dma((CHUNKS,)), dma, dma, dma, dma,
            dma((2,)), dma((CHUNKS,)), dma((2,)), dma((2, CHUNKS)), dma((2,)), dma((2, CHUNKS)),
            dma((2,)), dma((2,)), dma((2, CHUNKS)),
            dma, dma((CHUNKS,)), dma((2, 2)), dma((2, 2)), dma((2, 2)), dma((2, 2)), dma, dma,
        ],
        compiler_params=pltpu.CompilerParams(
            collective_id=0, has_side_effects=True, vmem_limit_bytes=56 * 1024 * 1024
        ),
        cost_estimate=pl.CostEstimate(flops=2 * 3 * 1024 * 2560 * 512, bytes_accessed=8 << 20, transcendentals=0),
    )(a_rows, a_cols, a_keep, b_rows, b_cols, a_blocks, b_blocks)


def solution(mesh):
    in_specs = (
        P(("row", "col"), None, None),
        P(("row", "col")),
        P(("row", "col")),
        P(("row", "col")),
        P(("row", "col"), None, None),
        P(("row", "col")),
        P(("row", "col")),
    )
    return jax.shard_map(
        on_device, mesh=mesh, in_specs=in_specs, out_specs=P("row", "col"), check_vma=False
    )
```

```python
import functools

import jax
import jax.numpy as jnp
from jax import lax
from jax.experimental import pallas as pl
from jax.experimental.pallas import tpu as pltpu
from jax.sharding import PartitionSpec as P

MESH = pl.DeviceIdType.MESH
BS = 64
KG = 64
RW = 2
CW = 8
SA = 20
SB = 64
PAIRS = SA // 2
ROWS = PAIRS * BS
PIECE = ROWS // 8
HALF = PIECE // 2
CHUNKS = 8
CROSS_LAST = (4, 5, 6)
BEFORE = (
    (("pass", 3), ("far", 1)),
    (("pass", 7), ("far", 2)),
    (("far", 3),),
    (("late", 4),),
    (("late", 5),),
    (("late", 6),),
    (("far", 7),),
    (),
)
LATE = len(CROSS_LAST)
UNROLL = 2
F32 = jnp.float32
BF16 = jnp.bfloat16


def split(value):
    high = value.astype(BF16)
    low = (value - high.astype(F32)).astype(BF16)
    return high, low


def kernel(
    a_rows, a_cols, a_keep, b_rows, b_cols, a_hbm, b_hbm, out,
    a_raw, packed, a_all, b_raw, twice_hi, twice_lo, dense_hi, dense_lo,
    meta_out, meta_in, meta_v, meta_s, table_v, table_s,
    c_part, z_half, z_full, c_x_out, c_x_in,
    load_sem, smem_sem, scat_send, scat_recv, meta_send, meta_recv, meta_swap_send, meta_swap_recv,
    x_send, x_recv, own_send, own_recv, near_send, near_recv, pass_send, pass_half_send, pass_recv,
    core_send, core_recv, zh_send, zh_recv, zf_send, zf_recv, h_send, h_recv,
):
    r = lax.axis_index("row")
    c = lax.axis_index("col")
    x_hi, z = r // 4, r % 4
    y, x_lo, core = c // 4, (c // 2) % 2, c % 2
    kappa, half = c % 8, c // 8
    local_target = jnp.logical_and(kappa == r, half == core)
    sibling = (r, y * 4 + x_lo * 2 + (1 - core))
    x_near = (r, y * 4 + (1 - x_lo) * 2 + core)
    y_way = [(r, ((y + 1) % 4) * 4 + x_lo * 2 + core), (r, ((y + 3) % 4) * 4 + x_lo * 2 + core)]
    z_way = [(x_hi * 4 + (z + 1) % 4, c), (x_hi * 4 + (z + 3) % 4, c)]
    x_far = ((1 - x_hi) * 4 + z, c)

    barrier = pltpu.get_barrier_semaphore()

    def greet(i, carry):
        @pl.when(jnp.logical_or(i != r, r + 8 * core != c))
        def _():
            pl.semaphore_signal(barrier, inc=1, device_id=(i, r + 8 * core), device_id_type=MESH)

        return carry

    lax.fori_loop(0, 8, greet, 0)
    for peer in (x_far, *z_way, *y_way, x_near, sibling):
        pl.semaphore_signal(barrier, inc=1, device_id=peer, device_id_type=MESH)

    load_a = pltpu.make_async_copy(a_hbm, a_raw, load_sem.at[0])
    load_b = pltpu.make_async_copy(b_hbm, b_raw, load_sem.at[1])
    load_a.start()
    load_b.start()

    lane = lax.broadcasted_iota(jnp.int32, (8, 128), 1)
    sub = lax.broadcasted_iota(jnp.int32, (8, 128), 0)
    meta = jnp.zeros((8, 128), jnp.int32)
    for a in range(SA):
        keep = a_keep[a]
        low_row = lax.rem(a_rows[a], RW)
        meta = jnp.where(lane == a, lax.rem(a_cols[a], KG) + half * KG, meta)
        meta = jnp.where(lane == 32 + a, keep * (1 - low_row), meta)
        meta = jnp.where(lane == 64 + a, keep * low_row, meta)
    meta_out[...] = meta

    load_a.wait()
    for p in range(PAIRS):
        packed[pl.ds(p * BS, BS), :] = jnp.concatenate([a_raw[2 * p], a_raw[2 * p + 1]], axis=1)

    @pl.when(local_target)
    def _():
        pl.semaphore_wait(barrier, 14)

    @pl.when(jnp.logical_not(local_target))
    def _():
        pl.semaphore_wait(barrier, 15)

    run = r * 2 + half

    def remote(src, dst, send, recv, peer):
        return pltpu.make_async_remote_copy(src, dst, send, recv, device_id=peer, device_id_type=MESH)

    def same(ref, send, recv, peer):
        return remote(ref, ref, send, recv, peer)

    def scatter(p, carry):
        target = (kappa, (p // 2) * 4 + (p % 2) * 2 + half)
        piece = packed.at[pl.ds(pl.multiple_of(p * PIECE, 16), PIECE)]
        place = a_all.at[run, p // 2, p % 2]
        here = jnp.logical_and(target[0] == r, target[1] == c)

        @pl.when(here)
        def _():
            pltpu.make_async_copy(piece, place, scat_recv.at[r]).start()
            pltpu.make_async_copy(meta_out, meta_in.at[r], meta_recv).start()

        @pl.when(jnp.logical_not(here))
        def _():
            remote(piece, place, scat_send, scat_recv.at[r], target).start()
            remote(meta_out, meta_in.at[r], meta_send, meta_recv, target).start()

        return carry

    lax.fori_loop(0, 8, scatter, 0)

    flat = sub * 128 + lane
    table = jnp.full((8, 128), SB, jnp.int32)
    for s in range(SB):
        inner = lax.rem(b_rows[s], KG) + (0 if s < SB // 2 else KG)
        place = inner * CW + lax.rem(b_cols[s], CW)
        table = jnp.where(flat == place, s, table)
    table_v[...] = table
    table_copy = pltpu.make_async_copy(table_v, table_s, smem_sem.at[0])
    table_copy.start()

    def rank(t):
        group = (t + 1) // 3
        return t - group * (2 - group) + 3 * ((t + 6) // 7 - (t + 5) // 7)

    def chunk_of(t):
        turn = rank(t) % 4
        away = (2 + turn + (turn // 2) * (5 - 2 * turn)) % 4
        return (x_hi + 1 - rank(t) // 4) % 2 * 4 + (z + away) % 4

    def plane(t):
        return a_all.at[2 * chunk_of(t) + core]

    def crosses_late(t):
        return t in CROSS_LAST

    def own(t):
        return plane(t).at[y, x_lo]

    def stage_own(t):
        piece = own(t)
        same(piece, own_send.at[0], scat_recv.at[chunk_of(t)], x_near).wait_recv()
        for way in range(2):
            same(piece, own_send.at[way], own_recv.at[way, t], y_way[way]).start()
        if not crosses_late(t):
            same(piece, x_send.at[0], x_recv.at[t], x_near).start()

    def stage_near(t):
        if not crosses_late(t):
            piece = plane(t).at[y, 1 - x_lo]
            same(piece, x_send.at[0], x_recv.at[t], x_near).wait_recv()
            for way in range(2):
                same(piece, near_send.at[way], near_recv.at[way, t], y_way[way]).start()

    def stage_pass(t):
        below = plane(t).at[(y + 3) % 4]
        above = plane(t).at[(y + 1) % 4]
        if crosses_late(t):
            for way, column in ((0, below), (1, above)):
                piece = column.at[x_lo]
                same(piece, own_send.at[way], own_recv.at[way, t], y_way[way]).wait_recv()
                part = piece.at[pl.ds(way * HALF, HALF)]
                same(part, pass_half_send.at[way], pass_recv.at[way, t], y_way[way]).start()
        else:
            same(below.at[x_lo], own_send.at[0], own_recv.at[0, t], y_way[0]).wait_recv()
            same(below.at[x_lo], pass_send.at[0], pass_recv.at[0, t], y_way[0]).start()
            same(above.at[1 - x_lo], near_send.at[1], near_recv.at[1, t], y_way[1]).wait_recv()
            same(above.at[1 - x_lo], pass_send.at[1], pass_recv.at[1, t], y_way[1]).start()

    def to_sibling(t):
        same(plane(t), core_send, core_recv.at[t], sibling).start()

    def stage_far(t):
        far = plane(t).at[(y + 2) % 4]
        if crosses_late(t):
            for way in range(2):
                part = far.at[x_lo, pl.ds(way * HALF, HALF)]
                same(part, pass_half_send.at[way], pass_recv.at[way, t], y_way[way]).wait_recv()
            same(plane(t).at[:, x_lo], x_send.at[1], x_recv.at[t], x_near).start()
        else:
            above = plane(t).at[(y + 1) % 4]
            below = plane(t).at[(y + 3) % 4]
            same(above.at[x_lo], own_send.at[1], own_recv.at[1, t], y_way[1]).wait_recv()
            same(below.at[1 - x_lo], near_send.at[0], near_recv.at[0, t], y_way[0]).wait_recv()
            same(far.at[x_lo], pass_send.at[0], pass_recv.at[0, t], y_way[0]).wait_recv()
            same(far.at[1 - x_lo], pass_send.at[1], pass_recv.at[1, t], y_way[1]).wait_recv()
            to_sibling(t)

    def stage_late(t):
        same(plane(t).at[:, 1 - x_lo], x_send.at[1], x_recv.at[t], x_near).wait_recv()
        to_sibling(t)

    pair_lane = lax.broadcasted_iota(jnp.int32, (1, 128), 1) < BS

    def pair_mask(h, ch, base, p):
        first = meta_s[h, ch, base + 2 * p].astype(F32)
        second = meta_s[h, ch, base + 2 * p + 1].astype(F32)
        return jnp.where(pair_lane, first, second)

    def pair_rows(at, p):
        parts, start, end = [], p * BS, (p + 1) * BS
        while start < end:
            piece, offset = divmod(start, PIECE)
            count = min(end - start, PIECE - offset)
            parts.append(a_all[at, piece // 2, piece % 2, pl.ds(offset, count), :])
            start += count
        return jnp.concatenate(parts, axis=0)

    def stage_product(t):
        ch = chunk_of(t)
        same(a_all.at[2 * ch + 1 - core], core_send, core_recv.at[t], sibling).wait_recv()
        total = jnp.zeros((RW * BS, CW * BS), F32)
        for h in range(2):
            for g in range(PAIRS // 2):
                block = jnp.concatenate([pair_rows(2 * ch + h, 2 * g + i) for i in range(2)], axis=1)
                high, low = split(block)
                masks = [
                    jnp.concatenate([pair_mask(h, ch, base, 2 * g + i) for i in range(2)], axis=1).astype(BF16)
                    for base in (32, 64)
                ]
                left_high = jnp.concatenate([high * m for m in masks], axis=0)
                left_low = jnp.concatenate([low * m for m in masks], axis=0)
                inner = [meta_s[h, ch, 4 * g + i] for i in range(4)]
                right_high = jnp.concatenate([dense_hi[k] for k in inner], axis=0)
                right_low = jnp.concatenate([dense_lo[k] for k in inner], axis=0)
                total += jnp.dot(left_high, right_high, preferred_element_type=F32)
                total += jnp.dot(left_low, right_high, preferred_element_type=F32)
                total += jnp.dot(left_high, right_low, preferred_element_type=F32)
        c_part[rank(t)] = total

    def part_rows(way):
        return pl.ds(way * BS, BS)

    def z_farthest(e, way):
        return remote(
            c_part.at[4 * e, part_rows(way)], z_half.at[e, way],
            zh_send.at[e, way], zh_recv.at[e, way], z_way[way],
        )

    def z_next(e, way, part):
        return remote(
            c_part.at[4 * e + 2 - way, part_rows(part)], z_full.at[e, way, part_rows(part)],
            zf_send.at[e, way, part], zf_recv.at[e, way, part], z_way[way],
        )

    def x_last(part):
        return remote(
            c_x_out.at[part_rows(part)], c_x_in.at[part_rows(part)], h_send.at[part], h_recv.at[part], x_far
        )

    def pass_along(e):
        for way in (1, 0):
            z_farthest(e, way).wait_recv()
            c_part[4 * e + 2 - way, part_rows(way), :] += z_half[e, way]
            for part in range(2):
                z_next(e, way, part).start()

    def arrived(e, part):
        for way in range(2):
            z_next(e, way, part).wait_recv()
        rows = part_rows(part)
        return c_part[4 * e + 3, rows, :] + z_full[e, 0, rows, :] + z_full[e, 1, rows, :]

    def sum_along(t):
        for e in range(2):
            @pl.when(t == e)
            def _():
                for way in range(2):
                    z_farthest(e, way).start()

        @pl.when(t == 3)
        def _():
            pass_along(0)

        @pl.when(t == 6)
        def _():
            pass_along(1)

        @pl.when(t == 6)
        def _():
            for part in range(2):
                c_x_out[part_rows(part), :] = arrived(0, part)
                x_last(part).start()

    first_half = lax.broadcasted_iota(jnp.int32, (BS, 2 * BS), 1) < BS

    def build(step, carry):
        for u in range(UNROLL):
            k = step * UNROLL + u
            slots = [table_s[k // 16, (k % 16) * CW + j] for j in range(CW)]
            for dense, twice in ((dense_hi, twice_hi), (dense_lo, twice_lo)):
                tiles = [
                    jnp.where(first_half, twice[slots[j]], twice[slots[j + 1]]) for j in range(0, CW, 2)
                ]
                dense[k] = jnp.concatenate(tiles, axis=1)
        return carry

    def build_some(start, end):
        lax.fori_loop(start // UNROLL, end // UNROLL, build, 0)

    load_b.wait()

    def widen(step, carry):
        for u in range(4):
            s = step * 4 + u
            value = b_raw[s]
            twice_hi[s], twice_lo[s] = split(jnp.concatenate([value, value], axis=1))
        return carry

    lax.fori_loop(0, SB // 4, widen, 0)
    for ref in (twice_hi, twice_lo):
        ref[SB] = jnp.zeros((BS, 2 * BS), BF16)

    def meta_pass_on():
        pltpu.make_async_copy(meta_in, meta_in, meta_recv).wait()
        for i in range(8):
            meta_v[core, pl.ds(i, 1), :] = meta_in[i, pl.ds(0, 1), :]
        same(meta_v.at[core], meta_swap_send, meta_swap_recv, sibling).start()

    meta_copy = pltpu.make_async_copy(meta_v, meta_s, smem_sem.at[1])

    def meta_take():
        same(meta_v.at[1 - core], meta_swap_send, meta_swap_recv, sibling).wait_recv()
        meta_copy.start()

    table_copy.wait()
    build_some(0, 64)
    stage_own(5)
    stage_own(6)
    stage_own(1)
    stage_own(4)
    stage_own(7)
    stage_own(2)
    stage_own(3)
    stage_own(0)
    meta_pass_on()
    stage_near(0)
    stage_near(1)
    build_some(64, 80)
    stage_pass(4)
    stage_pass(5)
    stage_pass(6)
    stage_near(2)
    stage_pass(0)
    build_some(80, 96)
    stage_near(3)
    stage_pass(1)
    build_some(96, 112)
    stage_far(4)
    stage_far(5)
    stage_far(6)
    stage_near(7)
    stage_pass(2)
    build_some(112, 128)
    meta_take()
    stage_far(0)
    meta_copy.wait()

    def step(i, carry):
        for at, stages in enumerate(BEFORE):
            @pl.when(i == at)
            def _():
                for stage, t in stages:
                    {"own": stage_own, "near": stage_near, "pass": stage_pass, "far": stage_far, "late": stage_late}[stage](t)

        stage_product(i)
        sum_along(i)
        return carry

    lax.fori_loop(0, CHUNKS, step, 0)

    for part in range(2):
        mine = arrived(1, part)
        x_last(part).wait_recv()
        out[part_rows(part), :] = mine + c_x_in[part_rows(part), :]

    def sent(ref, sem):
        remote(ref, ref, sem, load_sem.at[0], x_far).wait_send()

    def some(count):
        return a_all.at[pl.ds(0, count), 0, 0]

    @pl.when(local_target)
    def _():
        sent(some(7), scat_send)
        sent(meta_in.at[pl.ds(0, 7)], meta_send)

    @pl.when(jnp.logical_not(local_target))
    def _():
        sent(some(8), scat_send)
        sent(meta_in, meta_send)

    sent(meta_v.at[core], meta_swap_send)
    sent(some(CHUNKS - LATE), x_send.at[0])
    sent(a_all.at[pl.ds(0, LATE), :, 0], x_send.at[1])
    for way in range(2):
        sent(some(CHUNKS), own_send.at[way])
        sent(some(CHUNKS - LATE), near_send.at[way])
        sent(some(CHUNKS - LATE), pass_send.at[way])
        sent(a_all.at[pl.ds(0, LATE), 0, 0, pl.ds(0, HALF)], pass_half_send.at[way])
        for e in range(2):
            z_farthest(e, way).wait_send()
            for part in range(2):
                z_next(e, way, part).wait_send()
    sent(a_all.at[pl.ds(0, CHUNKS)], core_send)
    for part in range(2):
        x_last(part).wait_send()


def on_device(a_blocks, a_rows, a_cols, a_keep, b_blocks, b_rows, b_cols):
    dma = pltpu.SemaphoreType.DMA
    return pl.pallas_call(
        kernel,
        out_shape=jax.ShapeDtypeStruct((RW * BS, CW * BS), F32),
        in_specs=[pl.BlockSpec(memory_space=pltpu.SMEM)] * 5 + [pl.BlockSpec(memory_space=pl.ANY)] * 2,
        out_specs=pl.BlockSpec(memory_space=pltpu.VMEM),
        scratch_shapes=[
            pltpu.VMEM((SA, BS, BS), F32),
            pltpu.VMEM((ROWS, 128), F32),
            pltpu.VMEM((16, 4, 2, PIECE, 128), F32),
            pltpu.VMEM((SB, BS, BS), F32),
            pltpu.VMEM((SB + 1, BS, 128), BF16),
            pltpu.VMEM((SB + 1, BS, 128), BF16),
            pltpu.VMEM((2 * KG, BS, CW * BS), BF16),
            pltpu.VMEM((2 * KG, BS, CW * BS), BF16),
            pltpu.VMEM((8, 128), jnp.int32),
            pltpu.VMEM((8, 8, 128), jnp.int32),
            pltpu.VMEM((2, 8, 128), jnp.int32),
            pltpu.SMEM((2, 8, 128), jnp.int32),
            pltpu.VMEM((8, 128), jnp.int32),
            pltpu.SMEM((8, 128), jnp.int32),
            pltpu.VMEM((CHUNKS, RW * BS, CW * BS), F32),
            pltpu.VMEM((2, 2, BS, CW * BS), F32),
            pltpu.VMEM((2, 2, RW * BS, CW * BS), F32),
            pltpu.VMEM((RW * BS, CW * BS), F32),
            pltpu.VMEM((RW * BS, CW * BS), F32),
            dma((2,)), dma((2,)), dma, dma((CHUNKS,)), dma, dma, dma, dma,
            dma((2,)), dma((CHUNKS,)), dma((2,)), dma((2, CHUNKS)), dma((2,)), dma((2, CHUNKS)),
            dma((2,)), dma((2,)), dma((2, CHUNKS)),
            dma, dma((CHUNKS,)), dma((2, 2)), dma((2, 2)), dma((2, 2, 2)), dma((2, 2, 2)), dma((2,)), dma((2,)),
        ],
        compiler_params=pltpu.CompilerParams(
            collective_id=0, has_side_effects=True, vmem_limit_bytes=56 * 1024 * 1024
        ),
        cost_estimate=pl.CostEstimate(flops=2 * 3 * 1024 * 2560 * 512, bytes_accessed=8 << 20, transcendentals=0),
    )(a_rows, a_cols, a_keep, b_rows, b_cols, a_blocks, b_blocks)


def solution(mesh):
    in_specs = (
        P(("row", "col"), None, None),
        P(("row", "col")),
        P(("row", "col")),
        P(("row", "col")),
        P(("row", "col"), None, None),
        P(("row", "col")),
        P(("row", "col")),
    )
    return jax.shard_map(
        on_device, mesh=mesh, in_specs=in_specs, out_specs=P("row", "col"), check_vma=False
    )
```

```python
import functools

import jax
import jax.numpy as jnp
from jax import lax
from jax.experimental import pallas as pl
from jax.experimental.pallas import tpu as pltpu
from jax.sharding import PartitionSpec as P

MESH = pl.DeviceIdType.MESH
BS = 64
KG = 64
RW = 2
CW = 8
SA = 20
SB = 64
PAIRS = SA // 2
ROWS = PAIRS * BS
PIECE = ROWS // 8
HALF = PIECE // 2
CHUNKS = 8
CROSS_LAST = (4, 5, 6)
BEFORE = (
    (("pass", 3), ("far", 1)),
    (("pass", 7), ("far", 2)),
    (("far", 3),),
    (("late", 4),),
    (("late", 5),),
    (("late", 6),),
    (("far", 7),),
    (),
)
LATE = len(CROSS_LAST)
UNROLL = 2
F32 = jnp.float32
BF16 = jnp.bfloat16


def split(value):
    high = value.astype(BF16)
    low = (value - high.astype(F32)).astype(BF16)
    return high, low


def kernel(
    a_rows, a_cols, a_keep, b_rows, b_cols, a_hbm, b_hbm, out,
    a_raw, packed, a_all, b_raw, twice_hi, twice_lo, dense_hi, dense_lo,
    meta_out, meta_in, meta_v, meta_s, table_v, table_s,
    c_part, z_half, z_full, c_x_out, c_x_in,
    load_sem, smem_sem, scat_send, scat_recv, meta_send, meta_recv, meta_swap_send, meta_swap_recv,
    x_send, x_recv, own_send, own_recv, near_send, near_recv, pass_send, pass_half_send, pass_recv,
    core_send, core_recv, zh_send, zh_recv, zf_send, zf_recv, h_send, h_recv,
):
    r = lax.axis_index("row")
    c = lax.axis_index("col")
    x_hi, z = r // 4, r % 4
    y, x_lo, core = c // 4, (c // 2) % 2, c % 2
    kappa, half = c % 8, c // 8
    local_target = jnp.logical_and(kappa == r, half == core)
    sibling = (r, y * 4 + x_lo * 2 + (1 - core))
    x_near = (r, y * 4 + (1 - x_lo) * 2 + core)
    y_way = [(r, ((y + 1) % 4) * 4 + x_lo * 2 + core), (r, ((y + 3) % 4) * 4 + x_lo * 2 + core)]
    z_way = [(x_hi * 4 + (z + 1) % 4, c), (x_hi * 4 + (z + 3) % 4, c)]
    x_far = ((1 - x_hi) * 4 + z, c)

    barrier = pltpu.get_barrier_semaphore()

    def greet(i, carry):
        @pl.when(jnp.logical_or(i != r, r + 8 * core != c))
        def _():
            pl.semaphore_signal(barrier, inc=1, device_id=(i, r + 8 * core), device_id_type=MESH)

        return carry

    lax.fori_loop(0, 8, greet, 0)
    for peer in (x_far, *z_way, *y_way, x_near, sibling):
        pl.semaphore_signal(barrier, inc=1, device_id=peer, device_id_type=MESH)

    load_a = pltpu.make_async_copy(a_hbm, a_raw, load_sem.at[0])
    load_b = pltpu.make_async_copy(b_hbm, b_raw, load_sem.at[1])
    load_a.start()
    load_b.start()

    load_a.wait()
    for p in range(PAIRS):
        packed[pl.ds(p * BS, BS), :] = jnp.concatenate([a_raw[2 * p], a_raw[2 * p + 1]], axis=1)

    @pl.when(local_target)
    def _():
        pl.semaphore_wait(barrier, 14)

    @pl.when(jnp.logical_not(local_target))
    def _():
        pl.semaphore_wait(barrier, 15)

    run = r * 2 + half

    def remote(src, dst, send, recv, peer):
        return pltpu.make_async_remote_copy(src, dst, send, recv, device_id=peer, device_id_type=MESH)

    def same(ref, send, recv, peer):
        return remote(ref, ref, send, recv, peer)

    def scatter(step, carry):
        p = (step + 2 * z + 4 * x_hi + y) % 8
        target = (kappa, (p // 2) * 4 + (p % 2) * 2 + half)
        piece = packed.at[pl.ds(pl.multiple_of(p * PIECE, 16), PIECE)]
        place = a_all.at[run, p // 2, p % 2]
        here = jnp.logical_and(target[0] == r, target[1] == c)

        @pl.when(here)
        def _():
            pltpu.make_async_copy(piece, place, scat_recv.at[r]).start()

        @pl.when(jnp.logical_not(here))
        def _():
            remote(piece, place, scat_send, scat_recv.at[r], target).start()

        return carry

    lax.fori_loop(0, 8, scatter, 0)

    lane = lax.broadcasted_iota(jnp.int32, (8, 128), 1)
    sub = lax.broadcasted_iota(jnp.int32, (8, 128), 0)
    meta = jnp.zeros((8, 128), jnp.int32)
    for a in range(SA):
        keep = a_keep[a]
        low_row = lax.rem(a_rows[a], RW)
        meta = jnp.where(lane == a, lax.rem(a_cols[a], KG) + half * KG, meta)
        meta = jnp.where(lane == 32 + a, keep * (1 - low_row), meta)
        meta = jnp.where(lane == 64 + a, keep * low_row, meta)
    meta_out[...] = meta

    def tell(p, carry):
        target = (kappa, (p // 2) * 4 + (p % 2) * 2 + half)
        here = jnp.logical_and(target[0] == r, target[1] == c)

        @pl.when(here)
        def _():
            pltpu.make_async_copy(meta_out, meta_in.at[r], meta_recv).start()

        @pl.when(jnp.logical_not(here))
        def _():
            remote(meta_out, meta_in.at[r], meta_send, meta_recv, target).start()

        return carry

    lax.fori_loop(0, 8, tell, 0)

    flat = sub * 128 + lane
    table = jnp.full((8, 128), SB, jnp.int32)
    for s in range(SB):
        inner = lax.rem(b_rows[s], KG) + (0 if s < SB // 2 else KG)
        place = inner * CW + lax.rem(b_cols[s], CW)
        table = jnp.where(flat == place, s, table)
    table_v[...] = table
    table_copy = pltpu.make_async_copy(table_v, table_s, smem_sem.at[0])
    table_copy.start()

    def rank(t):
        group = (t + 1) // 3
        return t - group * (2 - group) + 3 * ((t + 6) // 7 - (t + 5) // 7)

    def chunk_of(t):
        turn = rank(t) % 4
        away = (2 + turn + (turn // 2) * (5 - 2 * turn)) % 4
        return (x_hi + 1 - rank(t) // 4) % 2 * 4 + (z + away) % 4

    def plane(t):
        return a_all.at[2 * chunk_of(t) + core]

    def crosses_late(t):
        return t in CROSS_LAST

    def own(t):
        return plane(t).at[y, x_lo]

    def stage_own(t):
        piece = own(t)
        same(piece, own_send.at[0], scat_recv.at[chunk_of(t)], x_near).wait_recv()
        for way in range(2):
            same(piece, own_send.at[way], own_recv.at[way, t], y_way[way]).start()
        if not crosses_late(t):
            same(piece, x_send.at[0], x_recv.at[t], x_near).start()

    def stage_near(t):
        if not crosses_late(t):
            piece = plane(t).at[y, 1 - x_lo]
            same(piece, x_send.at[0], x_recv.at[t], x_near).wait_recv()
            for way in range(2):
                same(piece, near_send.at[way], near_recv.at[way, t], y_way[way]).start()

    def stage_pass(t):
        below = plane(t).at[(y + 3) % 4]
        above = plane(t).at[(y + 1) % 4]
        if crosses_late(t):
            for way, column in ((0, below), (1, above)):
                piece = column.at[x_lo]
                same(piece, own_send.at[way], own_recv.at[way, t], y_way[way]).wait_recv()
                part = piece.at[pl.ds(way * HALF, HALF)]
                same(part, pass_half_send.at[way], pass_recv.at[way, t], y_way[way]).start()
        else:
            same(below.at[x_lo], own_send.at[0], own_recv.at[0, t], y_way[0]).wait_recv()
            same(below.at[x_lo], pass_send.at[0], pass_recv.at[0, t], y_way[0]).start()
            same(above.at[1 - x_lo], near_send.at[1], near_recv.at[1, t], y_way[1]).wait_recv()
            same(above.at[1 - x_lo], pass_send.at[1], pass_recv.at[1, t], y_way[1]).start()

    def to_sibling(t):
        same(plane(t), core_send, core_recv.at[t], sibling).start()

    def stage_far(t):
        far = plane(t).at[(y + 2) % 4]
        if crosses_late(t):
            for way in range(2):
                part = far.at[x_lo, pl.ds(way * HALF, HALF)]
                same(part, pass_half_send.at[way], pass_recv.at[way, t], y_way[way]).wait_recv()
            same(plane(t).at[:, x_lo], x_send.at[1], x_recv.at[t], x_near).start()
        else:
            above = plane(t).at[(y + 1) % 4]
            below = plane(t).at[(y + 3) % 4]
            same(above.at[x_lo], own_send.at[1], own_recv.at[1, t], y_way[1]).wait_recv()
            same(below.at[1 - x_lo], near_send.at[0], near_recv.at[0, t], y_way[0]).wait_recv()
            same(far.at[x_lo], pass_send.at[0], pass_recv.at[0, t], y_way[0]).wait_recv()
            same(far.at[1 - x_lo], pass_send.at[1], pass_recv.at[1, t], y_way[1]).wait_recv()
            to_sibling(t)

    def stage_late(t):
        same(plane(t).at[:, 1 - x_lo], x_send.at[1], x_recv.at[t], x_near).wait_recv()
        to_sibling(t)

    pair_lane = lax.broadcasted_iota(jnp.int32, (1, 128), 1) < BS

    def pair_mask(h, ch, base, p):
        first = meta_s[h, ch, base + 2 * p].astype(F32)
        second = meta_s[h, ch, base + 2 * p + 1].astype(F32)
        return jnp.where(pair_lane, first, second)

    def pair_rows(at, p):
        parts, start, end = [], p * BS, (p + 1) * BS
        while start < end:
            piece, offset = divmod(start, PIECE)
            count = min(end - start, PIECE - offset)
            parts.append(a_all[at, piece // 2, piece % 2, pl.ds(offset, count), :])
            start += count
        return jnp.concatenate(parts, axis=0)

    def stage_product(t):
        ch = chunk_of(t)
        same(a_all.at[2 * ch + 1 - core], core_send, core_recv.at[t], sibling).wait_recv()
        total = jnp.zeros((RW * BS, CW * BS), F32)
        for h in range(2):
            for g in range(PAIRS // 2):
                block = jnp.concatenate([pair_rows(2 * ch + h, 2 * g + i) for i in range(2)], axis=1)
                high, low = split(block)
                masks = [
                    jnp.concatenate([pair_mask(h, ch, base, 2 * g + i) for i in range(2)], axis=1).astype(BF16)
                    for base in (32, 64)
                ]
                left_high = jnp.concatenate([high * m for m in masks], axis=0)
                left_low = jnp.concatenate([low * m for m in masks], axis=0)
                inner = [meta_s[h, ch, 4 * g + i] for i in range(4)]
                right_high = jnp.concatenate([dense_hi[k] for k in inner], axis=0)
                right_low = jnp.concatenate([dense_lo[k] for k in inner], axis=0)
                total += jnp.dot(left_high, right_high, preferred_element_type=F32)
                total += jnp.dot(left_low, right_high, preferred_element_type=F32)
                total += jnp.dot(left_high, right_low, preferred_element_type=F32)
        c_part[rank(t)] = total

    def part_rows(way):
        return pl.ds(way * BS, BS)

    def z_farthest(e, way):
        return remote(
            c_part.at[4 * e, part_rows(way)], z_half.at[e, way],
            zh_send.at[e, way], zh_recv.at[e, way], z_way[way],
        )

    def z_next(e, way, part):
        return remote(
            c_part.at[4 * e + 2 - way, part_rows(part)], z_full.at[e, way, part_rows(part)],
            zf_send.at[e, way, part], zf_recv.at[e, way, part], z_way[way],
        )

    def x_last(part):
        return remote(
            c_x_out.at[part_rows(part)], c_x_in.at[part_rows(part)], h_send.at[part], h_recv.at[part], x_far
        )

    def pass_along(e):
        for way in (1, 0):
            z_farthest(e, way).wait_recv()
            c_part[4 * e + 2 - way, part_rows(way), :] += z_half[e, way]
            for part in ((way,) if e in (1,) else range(2)):
                z_next(e, way, part).start()

    def arrived(e, part):
        for way in range(2):
            z_next(e, way, part).wait_recv()
        rows = part_rows(part)
        return c_part[4 * e + 3, rows, :] + z_full[e, 0, rows, :] + z_full[e, 1, rows, :]

    def sum_along(t):
        for e in range(2):
            @pl.when(t == e)
            def _():
                for way in range(2):
                    z_farthest(e, way).start()

        for e, way, turn in ((1, 1, 5), (1, 0, 6), ):
            @pl.when(t == turn)
            def _():
                z_next(e, way, 1 - way).start()

        @pl.when(t == 3)
        def _():
            pass_along(0)

        @pl.when(t == 6)
        def _():
            pass_along(1)

        @pl.when(t == 6)
        def _():
            for part in range(2):
                c_x_out[part_rows(part), :] = arrived(0, part)
                x_last(part).start()

    first_half = lax.broadcasted_iota(jnp.int32, (BS, 2 * BS), 1) < BS

    def build(step, carry):
        for u in range(UNROLL):
            k = step * UNROLL + u
            slots = [table_s[k // 16, (k % 16) * CW + j] for j in range(CW)]
            for dense, twice in ((dense_hi, twice_hi), (dense_lo, twice_lo)):
                tiles = [
                    jnp.where(first_half, twice[slots[j]], twice[slots[j + 1]]) for j in range(0, CW, 2)
                ]
                dense[k] = jnp.concatenate(tiles, axis=1)
        return carry

    def build_some(start, end):
        lax.fori_loop(start // UNROLL, end // UNROLL, build, 0)

    load_b.wait()

    def widen(step, carry):
        for u in range(4):
            s = step * 4 + u
            value = b_raw[s]
            twice_hi[s], twice_lo[s] = split(jnp.concatenate([value, value], axis=1))
        return carry

    lax.fori_loop(0, SB // 4, widen, 0)
    for ref in (twice_hi, twice_lo):
        ref[SB] = jnp.zeros((BS, 2 * BS), BF16)

    def meta_pass_on():
        pltpu.make_async_copy(meta_in, meta_in, meta_recv).wait()
        for i in range(8):
            meta_v[core, pl.ds(i, 1), :] = meta_in[i, pl.ds(0, 1), :]
        same(meta_v.at[core], meta_swap_send, meta_swap_recv, sibling).start()

    meta_copy = pltpu.make_async_copy(meta_v, meta_s, smem_sem.at[1])

    def meta_take():
        same(meta_v.at[1 - core], meta_swap_send, meta_swap_recv, sibling).wait_recv()
        meta_copy.start()

    table_copy.wait()
    build_some(0, 64)
    stage_own(5)
    stage_own(6)
    stage_own(1)
    stage_own(4)
    stage_own(7)
    stage_own(2)
    stage_own(3)
    stage_own(0)
    meta_pass_on()
    stage_near(0)
    stage_near(1)
    stage_pass(4)
    stage_pass(5)
    stage_pass(6)
    build_some(64, 80)
    stage_near(2)
    stage_pass(0)
    build_some(80, 96)
    stage_near(3)
    stage_pass(1)
    stage_far(4)
    stage_far(5)
    stage_far(6)
    build_some(96, 112)
    stage_near(7)
    stage_pass(2)
    build_some(112, 128)
    meta_take()
    stage_far(0)
    meta_copy.wait()

    def step(i, carry):
        for at, stages in enumerate(BEFORE):
            @pl.when(i == at)
            def _():
                for stage, t in stages:
                    {"own": stage_own, "near": stage_near, "pass": stage_pass, "far": stage_far, "late": stage_late}[stage](t)

        stage_product(i)
        sum_along(i)
        return carry

    lax.fori_loop(0, CHUNKS, step, 0)

    for part in range(2):
        mine = arrived(1, part)
        x_last(part).wait_recv()
        out[part_rows(part), :] = mine + c_x_in[part_rows(part), :]

    def sent(ref, sem):
        remote(ref, ref, sem, load_sem.at[0], x_far).wait_send()

    def some(count):
        return a_all.at[pl.ds(0, count), 0, 0]

    @pl.when(local_target)
    def _():
        sent(some(7), scat_send)
        sent(meta_in.at[pl.ds(0, 7)], meta_send)

    @pl.when(jnp.logical_not(local_target))
    def _():
        sent(some(8), scat_send)
        sent(meta_in, meta_send)

    sent(meta_v.at[core], meta_swap_send)
    sent(some(CHUNKS - LATE), x_send.at[0])
    sent(a_all.at[pl.ds(0, LATE), :, 0], x_send.at[1])
    for way in range(2):
        sent(some(CHUNKS), own_send.at[way])
        sent(some(CHUNKS - LATE), near_send.at[way])
        sent(some(CHUNKS - LATE), pass_send.at[way])
        sent(a_all.at[pl.ds(0, LATE), 0, 0, pl.ds(0, HALF)], pass_half_send.at[way])
        for e in range(2):
            z_farthest(e, way).wait_send()
            for part in range(2):
                z_next(e, way, part).wait_send()
    sent(a_all.at[pl.ds(0, CHUNKS)], core_send)
    for part in range(2):
        x_last(part).wait_send()


def on_device(a_blocks, a_rows, a_cols, a_keep, b_blocks, b_rows, b_cols):
    dma = pltpu.SemaphoreType.DMA
    return pl.pallas_call(
        kernel,
        out_shape=jax.ShapeDtypeStruct((RW * BS, CW * BS), F32),
        in_specs=[pl.BlockSpec(memory_space=pltpu.SMEM)] * 5 + [pl.BlockSpec(memory_space=pl.ANY)] * 2,
        out_specs=pl.BlockSpec(memory_space=pltpu.VMEM),
        scratch_shapes=[
            pltpu.VMEM((SA, BS, BS), F32),
            pltpu.VMEM((ROWS, 128), F32),
            pltpu.VMEM((16, 4, 2, PIECE, 128), F32),
            pltpu.VMEM((SB, BS, BS), F32),
            pltpu.VMEM((SB + 1, BS, 128), BF16),
            pltpu.VMEM((SB + 1, BS, 128), BF16),
            pltpu.VMEM((2 * KG, BS, CW * BS), BF16),
            pltpu.VMEM((2 * KG, BS, CW * BS), BF16),
            pltpu.VMEM((8, 128), jnp.int32),
            pltpu.VMEM((8, 8, 128), jnp.int32),
            pltpu.VMEM((2, 8, 128), jnp.int32),
            pltpu.SMEM((2, 8, 128), jnp.int32),
            pltpu.VMEM((8, 128), jnp.int32),
            pltpu.SMEM((8, 128), jnp.int32),
            pltpu.VMEM((CHUNKS, RW * BS, CW * BS), F32),
            pltpu.VMEM((2, 2, BS, CW * BS), F32),
            pltpu.VMEM((2, 2, RW * BS, CW * BS), F32),
            pltpu.VMEM((RW * BS, CW * BS), F32),
            pltpu.VMEM((RW * BS, CW * BS), F32),
            dma((2,)), dma((2,)), dma, dma((CHUNKS,)), dma, dma, dma, dma,
            dma((2,)), dma((CHUNKS,)), dma((2,)), dma((2, CHUNKS)), dma((2,)), dma((2, CHUNKS)),
            dma((2,)), dma((2,)), dma((2, CHUNKS)),
            dma, dma((CHUNKS,)), dma((2, 2)), dma((2, 2)), dma((2, 2, 2)), dma((2, 2, 2)), dma((2,)), dma((2,)),
        ],
        compiler_params=pltpu.CompilerParams(
            collective_id=0, has_side_effects=True, vmem_limit_bytes=56 * 1024 * 1024
        ),
        cost_estimate=pl.CostEstimate(flops=2 * 3 * 1024 * 2560 * 512, bytes_accessed=8 << 20, transcendentals=0),
    )(a_rows, a_cols, a_keep, b_rows, b_cols, a_blocks, b_blocks)


def solution(mesh):
    in_specs = (
        P(("row", "col"), None, None),
        P(("row", "col")),
        P(("row", "col")),
        P(("row", "col")),
        P(("row", "col"), None, None),
        P(("row", "col")),
        P(("row", "col")),
    )
    return jax.shard_map(
        on_device, mesh=mesh, in_specs=in_specs, out_specs=P("row", "col"), check_vma=False
    )
```

```python
import functools

import jax
import jax.numpy as jnp
from jax import lax
from jax.experimental import pallas as pl
from jax.experimental.pallas import tpu as pltpu
from jax.sharding import PartitionSpec as P

MESH = pl.DeviceIdType.MESH
BS = 64
KG = 64
RW = 2
CW = 8
SA = 20
SB = 64
PAIRS = SA // 2
ROWS = PAIRS * BS
PIECE = ROWS // 8
HALF = PIECE // 2
CHUNKS = 8
CROSS_LAST = (4, 5, 6)
BEFORE = (
    (("pass", 3), ("far", 1)),
    (("pass", 7), ("far", 2)),
    (("far", 3),),
    (("late", 4),),
    (("late", 5),),
    (("late", 6),),
    (("far", 7),),
    (),
)
LATE = len(CROSS_LAST)
UNROLL = 2
F32 = jnp.float32
BF16 = jnp.bfloat16


def split(value):
    high = value.astype(BF16)
    low = (value - high.astype(F32)).astype(BF16)
    return high, low


def kernel(
    a_rows, a_cols, a_keep, b_rows, b_cols, a_hbm, b_hbm, out,
    a_raw, packed, a_all, b_raw, twice_hi, twice_lo, dense_hi, dense_lo,
    meta_out, meta_in, meta_v, meta_s, table_v, table_s,
    c_part, z_half, z_full, c_x_out, c_x_in,
    load_sem, smem_sem, scat_send, scat_recv, meta_send, meta_recv, meta_swap_send, meta_swap_recv,
    x_send, x_recv, own_send, own_recv, near_send, near_recv, pass_send, pass_half_send, pass_recv,
    core_send, core_recv, zh_send, zh_recv, zf_send, zf_recv, h_send, h_recv,
):
    r = lax.axis_index("row")
    c = lax.axis_index("col")
    x_hi, z = r // 4, r % 4
    y, x_lo, core = c // 4, (c // 2) % 2, c % 2
    kappa, half = c % 8, c // 8
    local_target = jnp.logical_and(kappa == r, half == core)
    sibling = (r, y * 4 + x_lo * 2 + (1 - core))
    x_near = (r, y * 4 + (1 - x_lo) * 2 + core)
    y_way = [(r, ((y + 1) % 4) * 4 + x_lo * 2 + core), (r, ((y + 3) % 4) * 4 + x_lo * 2 + core)]
    z_way = [(x_hi * 4 + (z + 1) % 4, c), (x_hi * 4 + (z + 3) % 4, c)]
    x_far = ((1 - x_hi) * 4 + z, c)

    barrier = pltpu.get_barrier_semaphore()

    def greet(i, carry):
        @pl.when(jnp.logical_or(i != r, r + 8 * core != c))
        def _():
            pl.semaphore_signal(barrier, inc=1, device_id=(i, r + 8 * core), device_id_type=MESH)

        return carry

    lax.fori_loop(0, 8, greet, 0)
    for peer in (x_far, *z_way, *y_way, x_near, sibling):
        pl.semaphore_signal(barrier, inc=1, device_id=peer, device_id_type=MESH)

    load_a = pltpu.make_async_copy(a_hbm, a_raw, load_sem.at[0])
    load_b = pltpu.make_async_copy(b_hbm, b_raw, load_sem.at[1])
    load_a.start()
    load_b.start()

    load_a.wait()
    for p in range(PAIRS):
        packed[pl.ds(p * BS, BS), :] = jnp.concatenate([a_raw[2 * p], a_raw[2 * p + 1]], axis=1)

    @pl.when(local_target)
    def _():
        pl.semaphore_wait(barrier, 14)

    @pl.when(jnp.logical_not(local_target))
    def _():
        pl.semaphore_wait(barrier, 15)

    run = r * 2 + half

    def remote(src, dst, send, recv, peer):
        return pltpu.make_async_remote_copy(src, dst, send, recv, device_id=peer, device_id_type=MESH)

    def same(ref, send, recv, peer):
        return remote(ref, ref, send, recv, peer)

    def scatter(step, carry):
        p = (step + 2 * z + 4 * x_hi + y) % 8
        target = (kappa, (p // 2) * 4 + (p % 2) * 2 + half)
        piece = packed.at[pl.ds(pl.multiple_of(p * PIECE, 16), PIECE)]
        place = a_all.at[run, p // 2, p % 2]
        here = jnp.logical_and(target[0] == r, target[1] == c)

        @pl.when(here)
        def _():
            pltpu.make_async_copy(piece, place, scat_recv.at[r]).start()

        @pl.when(jnp.logical_not(here))
        def _():
            remote(piece, place, scat_send, scat_recv.at[r], target).start()

        return carry

    lax.fori_loop(0, 8, scatter, 0)

    lane = lax.broadcasted_iota(jnp.int32, (8, 128), 1)
    sub = lax.broadcasted_iota(jnp.int32, (8, 128), 0)
    meta = jnp.zeros((8, 128), jnp.int32)
    for a in range(SA):
        keep = a_keep[a]
        low_row = lax.rem(a_rows[a], RW)
        meta = jnp.where(lane == a, lax.rem(a_cols[a], KG) + half * KG, meta)
        meta = jnp.where(lane == 32 + a, keep * (1 - low_row), meta)
        meta = jnp.where(lane == 64 + a, keep * low_row, meta)
    meta_out[...] = meta

    def tell(p, carry):
        target = (kappa, (p // 2) * 4 + (p % 2) * 2 + half)
        here = jnp.logical_and(target[0] == r, target[1] == c)

        @pl.when(here)
        def _():
            pltpu.make_async_copy(meta_out, meta_in.at[r], meta_recv).start()

        @pl.when(jnp.logical_not(here))
        def _():
            remote(meta_out, meta_in.at[r], meta_send, meta_recv, target).start()

        return carry

    lax.fori_loop(0, 8, tell, 0)

    flat = sub * 128 + lane
    table = jnp.full((8, 128), SB, jnp.int32)
    for s in range(SB):
        inner = lax.rem(b_rows[s], KG) + (0 if s < SB // 2 else KG)
        place = inner * CW + lax.rem(b_cols[s], CW)
        table = jnp.where(flat == place, s, table)
    table_v[...] = table
    table_copy = pltpu.make_async_copy(table_v, table_s, smem_sem.at[0])
    table_copy.start()

    def rank(t):
        group = (t + 1) // 3
        return t - group * (2 - group) + 3 * ((t + 6) // 7 - (t + 5) // 7)

    def chunk_of(t):
        turn = rank(t) % 4
        away = (2 + turn + (turn // 2) * (5 - 2 * turn)) % 4
        return (x_hi + 1 - rank(t) // 4) % 2 * 4 + (z + away) % 4

    def plane(t):
        return a_all.at[2 * chunk_of(t) + core]

    def crosses_late(t):
        return t in CROSS_LAST

    def own(t):
        return plane(t).at[y, x_lo]

    def stage_own(t):
        piece = own(t)
        same(piece, own_send.at[0], scat_recv.at[chunk_of(t)], x_near).wait_recv()
        for way in range(2):
            same(piece, own_send.at[way], own_recv.at[way, t], y_way[way]).start()
        if not crosses_late(t):
            same(piece, x_send.at[0], x_recv.at[t], x_near).start()

    def stage_near(t):
        if not crosses_late(t):
            piece = plane(t).at[y, 1 - x_lo]
            same(piece, x_send.at[0], x_recv.at[t], x_near).wait_recv()
            for way in range(2):
                same(piece, near_send.at[way], near_recv.at[way, t], y_way[way]).start()

    def stage_pass(t):
        below = plane(t).at[(y + 3) % 4]
        above = plane(t).at[(y + 1) % 4]
        if crosses_late(t):
            for way, column in ((0, below), (1, above)):
                piece = column.at[x_lo]
                same(piece, own_send.at[way], own_recv.at[way, t], y_way[way]).wait_recv()
                part = piece.at[pl.ds(way * HALF, HALF)]
                same(part, pass_half_send.at[way], pass_recv.at[way, t], y_way[way]).start()
        else:
            same(below.at[x_lo], own_send.at[0], own_recv.at[0, t], y_way[0]).wait_recv()
            same(below.at[x_lo], pass_send.at[0], pass_recv.at[0, t], y_way[0]).start()
            same(above.at[1 - x_lo], near_send.at[1], near_recv.at[1, t], y_way[1]).wait_recv()
            same(above.at[1 - x_lo], pass_send.at[1], pass_recv.at[1, t], y_way[1]).start()

    def to_sibling(t):
        same(plane(t), core_send, core_recv.at[t], sibling).start()

    def stage_far(t):
        far = plane(t).at[(y + 2) % 4]
        if crosses_late(t):
            for way in range(2):
                part = far.at[x_lo, pl.ds(way * HALF, HALF)]
                same(part, pass_half_send.at[way], pass_recv.at[way, t], y_way[way]).wait_recv()
            same(plane(t).at[:, x_lo], x_send.at[1], x_recv.at[t], x_near).start()
        else:
            above = plane(t).at[(y + 1) % 4]
            below = plane(t).at[(y + 3) % 4]
            same(above.at[x_lo], own_send.at[1], own_recv.at[1, t], y_way[1]).wait_recv()
            same(below.at[1 - x_lo], near_send.at[0], near_recv.at[0, t], y_way[0]).wait_recv()
            same(far.at[x_lo], pass_send.at[0], pass_recv.at[0, t], y_way[0]).wait_recv()
            same(far.at[1 - x_lo], pass_send.at[1], pass_recv.at[1, t], y_way[1]).wait_recv()
            to_sibling(t)

    def stage_late(t):
        same(plane(t).at[:, 1 - x_lo], x_send.at[1], x_recv.at[t], x_near).wait_recv()
        to_sibling(t)

    pair_lane = lax.broadcasted_iota(jnp.int32, (1, 128), 1) < BS

    def pair_mask(h, ch, base, p):
        first = meta_s[h, ch, base + 2 * p].astype(F32)
        second = meta_s[h, ch, base + 2 * p + 1].astype(F32)
        return jnp.where(pair_lane, first, second)

    def pair_rows(at, p):
        parts, start, end = [], p * BS, (p + 1) * BS
        while start < end:
            piece, offset = divmod(start, PIECE)
            count = min(end - start, PIECE - offset)
            parts.append(a_all[at, piece // 2, piece % 2, pl.ds(offset, count), :])
            start += count
        return jnp.concatenate(parts, axis=0)

    def stage_product(t):
        ch = chunk_of(t)
        same(a_all.at[2 * ch + 1 - core], core_send, core_recv.at[t], sibling).wait_recv()
        total = jnp.zeros((RW * BS, CW * BS), F32)
        for h in range(2):
            for g in range(PAIRS // 2):
                block = jnp.concatenate([pair_rows(2 * ch + h, 2 * g + i) for i in range(2)], axis=1)
                high, low = split(block)
                masks = [
                    jnp.concatenate([pair_mask(h, ch, base, 2 * g + i) for i in range(2)], axis=1).astype(BF16)
                    for base in (32, 64)
                ]
                left_high = jnp.concatenate([high * m for m in masks], axis=0)
                left_low = jnp.concatenate([low * m for m in masks], axis=0)
                inner = [meta_s[h, ch, 4 * g + i] for i in range(4)]
                right_high = jnp.concatenate([dense_hi[k] for k in inner], axis=0)
                right_low = jnp.concatenate([dense_lo[k] for k in inner], axis=0)
                total += jnp.dot(left_high, right_high, preferred_element_type=F32)
                total += jnp.dot(left_low, right_high, preferred_element_type=F32)
                total += jnp.dot(left_high, right_low, preferred_element_type=F32)
        c_part[rank(t)] = total

    def part_rows(way):
        return pl.ds(way * BS, BS)

    def z_farthest(e, way):
        return remote(
            c_part.at[4 * e, part_rows(way)], z_half.at[e, way],
            zh_send.at[e, way], zh_recv.at[e, way], z_way[way],
        )

    def z_next(e, way, part):
        return remote(
            c_part.at[4 * e + 2 - way, part_rows(part)], z_full.at[e, way, part_rows(part)],
            zf_send.at[e, way, part], zf_recv.at[e, way, part], z_way[way],
        )

    def x_last(part):
        return remote(
            c_x_out.at[part_rows(part)], c_x_in.at[part_rows(part)], h_send.at[part], h_recv.at[part], x_far
        )

    def pass_along(e):
        for way in (1, 0):
            z_farthest(e, way).wait_recv()
            c_part[4 * e + 2 - way, part_rows(way), :] += z_half[e, way]
            for part in ((way,) if e in (1,) else range(2)):
                z_next(e, way, part).start()

    def arrived(e, part):
        for way in range(2):
            z_next(e, way, part).wait_recv()
        rows = part_rows(part)
        return c_part[4 * e + 3, rows, :] + z_full[e, 0, rows, :] + z_full[e, 1, rows, :]

    def sum_along(t):
        for e in range(2):
            @pl.when(t == e)
            def _():
                for way in range(2):
                    z_farthest(e, way).start()

        for e, way, turn in ((1, 1, 5), (1, 0, 6), ):
            @pl.when(t == turn)
            def _():
                z_next(e, way, 1 - way).start()

        @pl.when(t == 3)
        def _():
            pass_along(0)

        @pl.when(t == 6)
        def _():
            pass_along(1)

        @pl.when(t == 6)
        def _():
            for part in range(2):
                c_x_out[part_rows(part), :] = arrived(0, part)
                x_last(part).start()

    first_half = lax.broadcasted_iota(jnp.int32, (BS, 2 * BS), 1) < BS

    def build(step, carry):
        for u in range(UNROLL):
            k = step * UNROLL + u
            slots = [table_s[k // 16, (k % 16) * CW + j] for j in range(CW)]
            for dense, twice in ((dense_hi, twice_hi), (dense_lo, twice_lo)):
                tiles = [
                    jnp.where(first_half, twice[slots[j]], twice[slots[j + 1]]) for j in range(0, CW, 2)
                ]
                dense[k] = jnp.concatenate(tiles, axis=1)
        return carry

    def build_some(start, end):
        lax.fori_loop(start // UNROLL, end // UNROLL, build, 0)

    load_b.wait()

    def widen(step, carry):
        for u in range(4):
            s = step * 4 + u
            value = b_raw[s]
            twice_hi[s], twice_lo[s] = split(jnp.concatenate([value, value], axis=1))
        return carry

    lax.fori_loop(0, SB // 4, widen, 0)
    for ref in (twice_hi, twice_lo):
        ref[SB] = jnp.zeros((BS, 2 * BS), BF16)

    def meta_pass_on():
        pltpu.make_async_copy(meta_in, meta_in, meta_recv).wait()
        for i in range(8):
            meta_v[core, pl.ds(i, 1), :] = meta_in[i, pl.ds(0, 1), :]
        same(meta_v.at[core], meta_swap_send, meta_swap_recv, sibling).start()

    meta_copy = pltpu.make_async_copy(meta_v, meta_s, smem_sem.at[1])

    def meta_take():
        same(meta_v.at[1 - core], meta_swap_send, meta_swap_recv, sibling).wait_recv()
        meta_copy.start()

    table_copy.wait()
    build_some(0, 32)
    stage_own(5)
    stage_own(6)
    stage_own(1)
    build_some(32, 48)
    stage_own(4)
    stage_own(7)
    build_some(48, 64)
    stage_own(2)
    stage_own(3)
    stage_own(0)
    meta_pass_on()
    stage_near(0)
    stage_near(1)
    build_some(64, 80)
    stage_pass(4)
    stage_pass(5)
    stage_pass(6)
    stage_near(2)
    stage_pass(0)
    build_some(80, 96)
    stage_near(3)
    stage_pass(1)
    build_some(96, 112)
    stage_far(4)
    stage_far(5)
    stage_far(6)
    stage_near(7)
    stage_pass(2)
    build_some(112, 128)
    meta_take()
    stage_far(0)
    meta_copy.wait()

    def step(i, carry):
        for at, stages in enumerate(BEFORE):
            @pl.when(i == at)
            def _():
                for stage, t in stages:
                    {"own": stage_own, "near": stage_near, "pass": stage_pass, "far": stage_far, "late": stage_late}[stage](t)

        stage_product(i)
        sum_along(i)
        return carry

    lax.fori_loop(0, CHUNKS, step, 0)

    for part in range(2):
        mine = arrived(1, part)
        x_last(part).wait_recv()
        out[part_rows(part), :] = mine + c_x_in[part_rows(part), :]

    def sent(ref, sem):
        remote(ref, ref, sem, load_sem.at[0], x_far).wait_send()

    def some(count):
        return a_all.at[pl.ds(0, count), 0, 0]

    @pl.when(local_target)
    def _():
        sent(some(7), scat_send)
        sent(meta_in.at[pl.ds(0, 7)], meta_send)

    @pl.when(jnp.logical_not(local_target))
    def _():
        sent(some(8), scat_send)
        sent(meta_in, meta_send)

    sent(meta_v.at[core], meta_swap_send)
    sent(some(CHUNKS - LATE), x_send.at[0])
    sent(a_all.at[pl.ds(0, LATE), :, 0], x_send.at[1])
    for way in range(2):
        sent(some(CHUNKS), own_send.at[way])
        sent(some(CHUNKS - LATE), near_send.at[way])
        sent(some(CHUNKS - LATE), pass_send.at[way])
        sent(a_all.at[pl.ds(0, LATE), 0, 0, pl.ds(0, HALF)], pass_half_send.at[way])
        for e in range(2):
            z_farthest(e, way).wait_send()
            for part in range(2):
                z_next(e, way, part).wait_send()
    sent(a_all.at[pl.ds(0, CHUNKS)], core_send)
    for part in range(2):
        x_last(part).wait_send()


def on_device(a_blocks, a_rows, a_cols, a_keep, b_blocks, b_rows, b_cols):
    dma = pltpu.SemaphoreType.DMA
    return pl.pallas_call(
        kernel,
        out_shape=jax.ShapeDtypeStruct((RW * BS, CW * BS), F32),
        in_specs=[pl.BlockSpec(memory_space=pltpu.SMEM)] * 5 + [pl.BlockSpec(memory_space=pl.ANY)] * 2,
        out_specs=pl.BlockSpec(memory_space=pltpu.VMEM),
        scratch_shapes=[
            pltpu.VMEM((SA, BS, BS), F32),
            pltpu.VMEM((ROWS, 128), F32),
            pltpu.VMEM((16, 4, 2, PIECE, 128), F32),
            pltpu.VMEM((SB, BS, BS), F32),
            pltpu.VMEM((SB + 1, BS, 128), BF16),
            pltpu.VMEM((SB + 1, BS, 128), BF16),
            pltpu.VMEM((2 * KG, BS, CW * BS), BF16),
            pltpu.VMEM((2 * KG, BS, CW * BS), BF16),
            pltpu.VMEM((8, 128), jnp.int32),
            pltpu.VMEM((8, 8, 128), jnp.int32),
            pltpu.VMEM((2, 8, 128), jnp.int32),
            pltpu.SMEM((2, 8, 128), jnp.int32),
            pltpu.VMEM((8, 128), jnp.int32),
            pltpu.SMEM((8, 128), jnp.int32),
            pltpu.VMEM((CHUNKS, RW * BS, CW * BS), F32),
            pltpu.VMEM((2, 2, BS, CW * BS), F32),
            pltpu.VMEM((2, 2, RW * BS, CW * BS), F32),
            pltpu.VMEM((RW * BS, CW * BS), F32),
            pltpu.VMEM((RW * BS, CW * BS), F32),
            dma((2,)), dma((2,)), dma, dma((CHUNKS,)), dma, dma, dma, dma,
            dma((2,)), dma((CHUNKS,)), dma((2,)), dma((2, CHUNKS)), dma((2,)), dma((2, CHUNKS)),
            dma((2,)), dma((2,)), dma((2, CHUNKS)),
            dma, dma((CHUNKS,)), dma((2, 2)), dma((2, 2)), dma((2, 2, 2)), dma((2, 2, 2)), dma((2,)), dma((2,)),
        ],
        compiler_params=pltpu.CompilerParams(
            collective_id=0, has_side_effects=True, vmem_limit_bytes=56 * 1024 * 1024
        ),
        cost_estimate=pl.CostEstimate(flops=2 * 3 * 1024 * 2560 * 512, bytes_accessed=8 << 20, transcendentals=0),
    )(a_rows, a_cols, a_keep, b_rows, b_cols, a_blocks, b_blocks)


def solution(mesh):
    in_specs = (
        P(("row", "col"), None, None),
        P(("row", "col")),
        P(("row", "col")),
        P(("row", "col")),
        P(("row", "col"), None, None),
        P(("row", "col")),
        P(("row", "col")),
    )
    return jax.shard_map(
        on_device, mesh=mesh, in_specs=in_specs, out_specs=P("row", "col"), check_vma=False
    )
```
